256 devices in a mesh: ctx: 64 (over x, y, z_hi, core), tp: 4 (over z_lo).
Axes of the slice: x: 4, y: 4, z: 8 (z_hi: 2, z_lo: 4; z = z_hi * 4 + z_lo), core: 2. Of those that a mesh axis runs over, the one named last changes fastest.
Arguments:
- stream: bfloat16 [4096, 8192], P('ctx', 'tp'), may hold values from -20 to 20
- se_pregate: bfloat16 [4096, 8192], P('ctx', 'tp'), may hold values from -6 to 6
- se_postgate: bfloat16 [4096, 8192], P('ctx', 'tp'), may hold values from -6 to 6
- se_taps: bfloat16 [8192, 7], P('tp'), may hold values from -2 to 2
- mr_pregate: bfloat16 [4096, 8192], P('ctx', 'tp'), may hold values from -6 to 6
- mr_postgate: bfloat16 [4096, 8192], P('ctx', 'tp'), may hold values from -6 to 6
- mr_taps: bfloat16 [16, 128], P('tp'), may hold values from -0.5 to 0.5
- query_rows: bfloat16 [4096, 4096], P('ctx', 'tp'), may hold values from -120 to 120
- key_rows: bfloat16 [4096, 4096], P('ctx', 'tp'), may hold values from -6 to 6
- value_rows: bfloat16 [4096, 4096], P('ctx', 'tp'), may hold values from -6 to 6
- block_owner: int32 [128, 1], replicated, may hold values from 0 to 63; in each aligned block of 128 rows (0 to 127, 128 to 255, ...) at most 4 rows name the same one
Outputs:
- hyena_stream: bfloat16 [4096, 8192], P('ctx', 'tp')
- attention_out: bfloat16 [4096, 4096], P('ctx', 'tp')
- decode_cache: bfloat16 [8192, 2, 4096], P('ctx', None, 'tp')
- filter_state: bfloat16 [8192, 8192], P('ctx', 'tp')
The draws below stay inside these ranges and needn't reach their ends.
Inputs may be any that keep to these rules, and one draw needn't show every extreme that they name: `block_owner`: no owner is named by more than 4 tiles; some owner is named by exactly 4.
All inputs are finite; a program needn't handle non-finite values.
Results may differ from the reference program's by a relative error of at most 0.007.
Values may be sent and summed in bfloat16 or wider, within the bound.
No kernel may reach another device: no remote copies, remote signals or barrier semaphores. Data moves between devices by JAX's collectives and lax.ppermute only.
A program may use at most 192 MiB of HBM per device.

```python
import math
import jax
import jax.numpy as jnp
import numpy as np
from jax import lax

D = 8192
HEADS = 32
HEAD_DIM = 128
GROUPS = 16
SE_TAPS = 7
MR_TAPS = 128
CAP = 4
TOK_DEV = 64
HALF = 32
TOKENS = 4096
N_CTX = 64


def draw_stream(key, part):
    key = jax.random.fold_in(key, 7)
    columns = jnp.arange(D, dtype=jnp.float32)
    rising = 0.6 * jnp.power(3.0, columns / D)
    values = jnp.clip(jax.random.normal(key, (TOKENS, D), jnp.float32), -6.0, 6.0) * rising[None, :]
    return values.astype(jnp.bfloat16)


def draw_query_rows(key, part):
    key = jax.random.fold_in(key, 11)
    base = jnp.clip(jax.random.normal(key, (TOKENS, HEADS * HEAD_DIM), jnp.float32), -6.0, 6.0)
    return base.astype(jnp.bfloat16)


def draw_key_rows(key, part):
    key = jax.random.fold_in(key, 13)
    base = jnp.clip(jax.random.normal(key, (TOKENS, HEADS * HEAD_DIM), jnp.float32), -6.0, 6.0)
    return base.astype(jnp.bfloat16)


def levels(key, extent, pieces, least, high):
    def one(dim, blocks):
        steps = jax.random.uniform(jax.random.fold_in(jax.random.fold_in(key, 6), dim), (blocks,), jnp.float32, least / len(pieces), high / len(pieces))
        return jnp.repeat(jnp.exp(steps), extent[dim] // blocks).reshape((-1,) + (1,) * (len(extent) - dim - 1))

    level = one(*pieces[0])
    for cut in pieces[1:]:
        level = level * one(*cut)
    return level


def assign_block(key, own, number, rows, amount, top, reach, slope):
    ranking = jax.random.permutation(key, amount)
    heavy_load, ordinary = portions_of(amount, rows * top, reach, slope, True), portions_of(amount, rows * top, reach, slope, False)
    places = jnp.arange(amount)

    def named(tallies, turn):
        used = int((tallies > 0).sum())
        fixed = max(1, used // 4)
        passed = fixed + (places - fixed + turn * (used - fixed)) % max(1, amount - fixed)
        return jnp.zeros((amount,), jnp.int32).at[ranking[jnp.where(places < fixed, places, passed)]].set(jnp.asarray(tallies, jnp.int32))

    tallies = jnp.where(number % 4 == 0, named(heavy_load, number // 4), named(ordinary, number - number // 4 - 1))
    mixed = jax.random.permutation(jax.random.fold_in(own, 3), amount)
    source_of, taker = mixed[0:amount // 2 * 2:2], mixed[1:amount // 2 * 2:2]
    slack = jnp.minimum(tallies[source_of] - 1, reach - tallies[taker]) // 2
    slack = jnp.where((source_of == ranking[0]) | (taker == ranking[0]) | (tallies[taker] == 0), 0, jnp.maximum(slack, 0))
    passed = jax.random.randint(jax.random.fold_in(own, 4), (amount // 2,), 0, 1 << 20) % (slack + 1)
    tallies = tallies.at[source_of].add(-passed).at[taker].add(passed)
    members = jnp.searchsorted(jnp.cumsum(tallies), jnp.arange(rows * top), side="right").astype(jnp.int32)
    grid = members.reshape(top, rows).T
    grid = grid[jax.random.permutation(jax.random.fold_in(own, 1), rows)]
    turn = jax.random.randint(jax.random.fold_in(own, 2), (rows, 1), 0, top)
    return jnp.take_along_axis(grid, (jnp.arange(top)[None, :] + turn) % top, axis=1)


def portions_of(amount, total, bound, slope, full):
    weights = [(1 << 20) // math.isqrt(rank ** slope) + 1 for rank in range(1, amount + 1)]
    largest = bound if full else min(bound, max(-(-total // amount), total * weights[0] // sum(weights)))
    least = 1 if total - largest >= amount - 1 else 0
    given, rest = [largest] + [least] * (amount - 1), total - largest - least * (amount - 1)
    while rest > 0:
        free = [i for i in range(1, amount) if given[i] < largest] or [i for i in range(1, amount) if given[i] < bound]
        pool, remaining = sum([weights[i] for i in free]), rest
        for i in free:
            extra = min(bound - given[i], max(1, remaining * weights[i] // pool), rest)
            given[i] = given[i] + extra
            rest = rest - extra
    return np.array(given)


def normal_values(rng, extent, scale, reach, pieces=(), held_as=jnp.bfloat16):
    result = jax.random.normal(rng, extent, jnp.float32) * scale
    if len(pieces) > 0:
        result = levels(rng, extent, pieces, -0.22, 0.18) * result
    return jnp.clip(result, min=-reach, max=reach).astype(held_as)


def setup_inputs(seed: int = 0) -> dict:
    seeds = jax.random.split(jax.random.key(seed), 12)
    stream = draw_stream(jax.random.fold_in(seeds[11], 71), 0)
    se_pregate = normal_values(seeds[1], (TOKENS, D), 1.0, 6.0, ((0, 64), (1, 4)))
    se_postgate = normal_values(seeds[2], (TOKENS, D), 1.0, 6.0, ((0, 64), (1, 4)))
    se_taps = normal_values(seeds[3], (D, SE_TAPS), SE_TAPS ** -0.5, 2.0, ((0, 4),))
    mr_pregate = normal_values(seeds[4], (TOKENS, D), 1.0, 6.0, ((0, 64), (1, 4)))
    mr_postgate = normal_values(seeds[5], (TOKENS, D), 1.0, 6.0, ((0, 64), (1, 4)))
    mr_taps = normal_values(seeds[6], (GROUPS, MR_TAPS), MR_TAPS ** -0.5, 0.5, ((0, 4),))
    query_rows = draw_query_rows(jax.random.fold_in(seeds[11], 71), 0)
    key_rows = draw_key_rows(jax.random.fold_in(seeds[11], 71), 0)
    value_rows = normal_values(seeds[9], (TOKENS, HEADS * HEAD_DIM), 1.0, 6.0, ((0, 64), (1, 4)))
    block_owner_keys = jax.random.split(jax.random.fold_in(seeds[10], 1), (2 * N_CTX) // (2 * N_CTX))
    block_owner_turns = jax.random.permutation(jax.random.fold_in(seeds[10], 3), (2 * N_CTX) // (2 * N_CTX))
    block_owner = jax.vmap(lambda own, number: assign_block(jax.random.fold_in(seeds[10], 2), own, number, 2 * N_CTX, N_CTX, 1, CAP, 2))(block_owner_keys, block_owner_turns).reshape((2 * N_CTX, 1))
    return {"stream": stream, "se_pregate": se_pregate, "se_postgate": se_postgate, "se_taps": se_taps, "mr_pregate": mr_pregate, "mr_postgate": mr_postgate, "mr_taps": mr_taps, "query_rows": query_rows, "key_rows": key_rows, "value_rows": value_rows, "block_owner": block_owner}


NEG_FILL = -1e+30
EPS_NORM = 1e-06

def mirror_place(count, tok_dev):
    rowid = jnp.arange(count * tok_dev, dtype=jnp.int32)
    device = rowid // tok_dev
    within = rowid % tok_dev
    half_rows = tok_dev // 2
    early = device * half_rows + within
    late = (2 * count - 1 - device) * half_rows + within - half_rows
    return jnp.where(within < half_rows, early, late).astype(jnp.int32)

def row_scale(signal):
    wide = signal.astype(jnp.float32)
    return lax.rsqrt(lax.optimization_barrier(jnp.mean(wide * wide, axis=1)) + EPS_NORM)

def causal_filter(signal, taps):
    width = taps.shape[1]
    length = signal.shape[0]
    padded = jnp.pad(signal, ((width - 1, 0), (0, 0)))

    def add_tap(index, total):
        start = (width - 1 - index).astype(jnp.int32)
        shifted = lax.dynamic_slice_in_dim(padded, start, length, 0)
        column = lax.dynamic_index_in_dim(taps, index.astype(jnp.int32), 1, keepdims=False)
        return total + column[None, :] * shifted
    return lax.fori_loop(0, width, add_tap, jnp.zeros(signal.shape, jnp.float32))

def reference(stream, se_pregate, se_postgate, se_taps, mr_pregate, mr_postgate, mr_taps, query_rows, key_rows, value_rows, block_owner):
    place = mirror_place(N_CTX, TOK_DEV)
    order = jnp.zeros((TOKENS,), jnp.int32).at[place].set(jnp.arange(TOKENS, dtype=jnp.int32))

    def to_seq(array):
        return jnp.take(array, order, axis=0)

    def to_store(array):
        return jnp.take(array, place, axis=0)
    stream_seq = to_seq(stream)
    scale_one = row_scale(stream_seq)
    se_input = lax.optimization_barrier((to_seq(se_pregate).astype(jnp.float32) * stream_seq.astype(jnp.float32) * scale_one[:, None]).astype(jnp.bfloat16))
    se_out = causal_filter(se_input.astype(jnp.float32), se_taps.astype(jnp.float32))
    mixed = lax.optimization_barrier((stream_seq.astype(jnp.float32) + to_seq(se_postgate).astype(jnp.float32) * se_out).astype(jnp.bfloat16))
    scale_two = row_scale(mixed)
    mr_input = lax.optimization_barrier((to_seq(mr_pregate).astype(jnp.float32) * mixed.astype(jnp.float32) * scale_two[:, None]).astype(jnp.bfloat16))
    per_channel = jnp.repeat(mr_taps.astype(jnp.float32), D // GROUPS, axis=0)
    mr_out = causal_filter(mr_input.astype(jnp.float32), per_channel)
    hyena_seq = (mixed.astype(jnp.float32) + to_seq(mr_postgate).astype(jnp.float32) * mr_out).astype(jnp.bfloat16)
    hyena_stream = to_store(hyena_seq)
    scale = 1.0 / math.sqrt(HEAD_DIM)
    spots = jnp.arange(TOKENS, dtype=jnp.int32)
    causal = spots[:, None] >= spots[None, :]

    def by_head(array):
        return to_seq(array).reshape(TOKENS, HEADS, HEAD_DIM).transpose(1, 0, 2)

    def one_head(parts):
        q_head, k_head, v_head = parts
        scores = jnp.dot(q_head, k_head.T, preferred_element_type=jnp.float32) * scale
        scores = jnp.where(causal, scores, NEG_FILL)
        top = lax.optimization_barrier(jnp.max(scores, axis=1, keepdims=True))
        weights = jnp.where(causal, jnp.exp(scores - top), 0.0)
        total = lax.optimization_barrier(jnp.sum(weights, axis=1, keepdims=True))
        summed = jnp.dot(weights.astype(jnp.bfloat16), v_head, preferred_element_type=jnp.float32)
        return summed / total
    heads_out = lax.map(one_head, (by_head(query_rows), by_head(key_rows), by_head(value_rows)))
    attention_seq = heads_out.transpose(1, 0, 2).reshape(TOKENS, HEADS * HEAD_DIM).astype(jnp.bfloat16)
    attention_out = to_store(attention_seq)
    owners = block_owner[:, 0].astype(jnp.int32)
    tiles_all = 2 * N_CTX
    tile_ids = jnp.arange(tiles_all, dtype=jnp.int32)
    earlier = tile_ids[:, None] > tile_ids[None, :]
    same = owners[:, None] == owners[None, :]
    ranks = lax.optimization_barrier(jnp.sum((earlier & same).astype(jnp.int32), axis=1))
    tile_of = spots // HALF
    target = ((owners[tile_of] * CAP + ranks[tile_of]) * HALF + spots % HALF).astype(jnp.int32)
    packed = jnp.stack([to_seq(key_rows), to_seq(value_rows)], axis=1)
    decode_cache = jnp.zeros((N_CTX * CAP * HALF, 2, HEADS * HEAD_DIM), jnp.bfloat16).at[target].set(packed)
    tail = mr_input[TOKENS - MR_TAPS:]
    filter_state = jnp.zeros((N_CTX * MR_TAPS, D), jnp.bfloat16).at[:MR_TAPS].set(tail)
    return (hyena_stream, attention_out, decode_cache, filter_state)
```

```python
import functools
import math

import jax
import jax.numpy as jnp
from jax import lax
from jax.experimental import pallas as pl
from jax.experimental.pallas import tpu as pltpu
from jax.sharding import Mesh, PartitionSpec as P

HEAD_DIM = 128
CAP = 4
EPS_NORM = 1e-06
MASKED = -1e30
CTX = ("x", "y", "zh", "c")
F32 = jnp.float32
BF16 = jnp.bfloat16
LANES = 128
TILE = 32
TAPS = 7
PAIRS = tuple((a, b) for a in range(TAPS + 1) for b in range(a, TAPS + 1))


def ctx_route(array, target):
    pairs = [(i, target(i)) for i in range(64) if 0 <= target(i) < 64]
    return lax.ppermute(array, CTX, pairs)


def call(kernel, out_shape, scratch=(), in_spaces=None, flops=0, nbytes=0, name=None):
    specs = [pl.BlockSpec(memory_space=space) for space in in_spaces]
    if isinstance(out_shape, (list, tuple)):
        outs = [pl.BlockSpec(memory_space=pltpu.VMEM) for _ in out_shape]
    else:
        outs = pl.BlockSpec(memory_space=pltpu.VMEM)
    return pl.pallas_call(
        kernel,
        out_shape=out_shape,
        in_specs=specs,
        out_specs=outs,
        scratch_shapes=list(scratch),
        compiler_params=pltpu.CompilerParams(vmem_limit_bytes=40 * 1024 * 1024),
        cost_estimate=pl.CostEstimate(flops=flops, bytes_accessed=nbytes, transcendentals=0),
        name=name,
    )


V, S = pltpu.VMEM, pltpu.SMEM


def lanes_at(index, width):
    return pl.ds(pl.multiple_of(index * width, width), width)


def halo_products(meta, stream, pre, he, hl, cs):
    last = meta[0] == 63
    s = stream[:, cs].astype(F32)
    u = s * pre[:, cs].astype(F32)
    early = he[:, cs].astype(F32)
    late = hl[:, cs].astype(F32)
    early_u = early[0:8] * early[8:16]
    late_s = jnp.where(last, s[TILE - 8 : TILE], late[0:8])
    late_u = jnp.where(last, u[TILE - 8 : TILE], late[0:8] * late[8:16])
    return s, u, early[0:8], early_u, late_s, late_u


def stats_kernel(meta, stream, pre, post, taps, he, hl, out, us, sf, pf):
    def prepare(step, carry):
        acc_e, acc_l = carry
        cs = lanes_at(step, LANES)
        s, u, es, eu, ls, lu = halo_products(meta, stream, pre, he, hl, cs)
        sf[:, cs] = s
        pf[:, cs] = post[:, cs].astype(F32)
        us[0, 0:8, cs] = eu
        us[0, 8:40, cs] = u[0:TILE]
        us[1, 0:8, cs] = lu
        us[1, 8:40, cs] = u[TILE:]
        return acc_e + es * es, acc_l + ls * ls

    chunks = stream.shape[1] // LANES
    zero = jnp.zeros((8, LANES), F32)
    acc_e, acc_l = lax.fori_loop(0, chunks, prepare, (zero, zero))
    lane = lax.broadcasted_iota(jnp.int32, (8, LANES), 1)
    out[64:72, :] = jnp.where(lane == 0, jnp.sum(acc_e, axis=1, keepdims=True), 0.0)
    out[72:80, :] = jnp.where(lane == 0, jnp.sum(acc_l, axis=1, keepdims=True), 0.0)
    for tile in range(2):
        for group in range(TILE // 8):
            row = tile * TILE + group * 8

            def collect(step, sums, tile=tile, group=group, row=row):
                cs = lanes_at(step, LANES)
                gate = pf[row : row + 8, cs]
                terms = [sf[row : row + 8, cs]]
                for j in range(TAPS):
                    behind = us[tile, pl.ds(group * 8 + 8 - j, 8), cs]
                    terms.append(taps[j : j + 1, cs] * gate * behind)
                return tuple(t + terms[a] * terms[b] for t, (a, b) in zip(sums, PAIRS))

            sums = lax.fori_loop(0, chunks, collect, (zero,) * len(PAIRS))
            packed = zero
            for q, part in enumerate(sums):
                packed = jnp.where(lane == q, jnp.sum(part, axis=1, keepdims=True), packed)
            out[row : row + 8, :] = packed


def mix_kernel(meta, stream, pre, post, taps, he, hl, total, mrpre, mixed, early, late, sc, s2, xs):
    width = 1.0 / 8192.0
    scale = lax.rsqrt(total[:, 0:1] * width + EPS_NORM)
    wide = jnp.broadcast_to(scale, (80, LANES))
    sc[0, 0:8, :] = wide[64:72]
    sc[0, 8:40, :] = wide[0:TILE]
    sc[1, 0:8, :] = wide[72:80]
    sc[1, 8:40, :] = wide[TILE:64]
    lane = lax.broadcasted_iota(jnp.int32, (TILE, LANES), 1)
    for tile in range(2):
        factor = [jnp.ones((TILE, LANES), F32)]
        for j in range(TAPS):
            factor.append(sc[tile, pl.ds(8 - j, TILE), :])
        weight = jnp.zeros((TILE, LANES), F32)
        for q, (a, b) in enumerate(PAIRS):
            term = factor[a] * factor[b]
            weight = jnp.where(lane == q, term if a == b else term * 2.0, weight)
        rows = slice(tile * TILE, (tile + 1) * TILE)
        squares = jnp.sum(weight * total[rows, :], axis=1, keepdims=True)
        second = lax.rsqrt(jnp.maximum(squares, 0.0) * width + EPS_NORM)
        s2[rows, :] = jnp.broadcast_to(second, (TILE, LANES))

    def one(step, carry):
        cs = lanes_at(step, LANES)
        s, u, _, eu, _, lu = halo_products(meta, stream, pre, he, hl, cs)
        gate = post[:, cs].astype(F32)
        front = mrpre[:, cs].astype(F32)
        for tile, halo in enumerate((eu, lu)):
            rows = slice(tile * TILE, (tile + 1) * TILE)
            xs[tile, 0:8, :] = (halo * sc[tile, 0:8, :]).astype(BF16).astype(F32)
            xs[tile, 8:40, :] = (u[rows] * sc[tile, 8:40, :]).astype(BF16).astype(F32)
        for tile, target in enumerate((early, late)):
            rows = slice(tile * TILE, (tile + 1) * TILE)
            acc = jnp.zeros((TILE, LANES), F32)
            for j in range(TAPS):
                acc = acc + taps[j : j + 1, cs] * xs[tile, pl.ds(8 - j, TILE), :]
            value = (s[rows] + gate[rows] * acc).astype(BF16)
            mixed[rows, cs] = value
            target[:, cs] = (front[rows] * value.astype(F32) * s2[rows, :]).astype(BF16)
        return carry

    lax.fori_loop(0, stream.shape[1] // LANES, one, 0)


def conv_kernel(meta, taps, mixed, post, early, late, e2, e4, l2, l4, swapped, out, state, ext):
    first = meta[0] == 0
    ext[0, 0:32, :] = e4[...]
    ext[0, 32:64, :] = swapped[1]
    ext[0, 64:96, :] = e2[...]
    ext[0, 96:128, :] = swapped[0]
    ext[0, 128:160, :] = early[...]
    ext[1, 0:32, :] = l4[...]
    ext[1, 32:64, :] = swapped[3]
    ext[1, 64:96, :] = l2[...]
    ext[1, 96:128, :] = swapped[2]
    ext[1, 128:160, :] = late[...]
    group_width = out.shape[1] // taps.shape[0]
    for g in range(taps.shape[0]):
        row = jnp.broadcast_to(taps[g : g + 1, :], (TILE, 256))
        toeplitz = pltpu.roll(row, 0, 1, stride=1, stride_axis=0)[:, 0:160].astype(BF16)
        cols = slice(g * group_width, (g + 1) * group_width)
        for tile in range(2):
            rows = slice(tile * TILE, (tile + 1) * TILE)
            acc = jnp.dot(toeplitz, ext[tile, :, cols], preferred_element_type=F32)
            value = mixed[rows, cols].astype(F32) + post[rows, cols].astype(F32) * acc
            out[rows, cols] = value.astype(BF16)

    @pl.when(first)
    def _():
        state[...] = ext[1, 32:160, :]

    @pl.when(jnp.logical_not(first))
    def _():
        state[...] = jnp.zeros_like(state)


def pack_kernel(meta, k, v, kz, vz, q, out):
    half = meta[2]
    for a in range(8):
        cols = slice(a * LANES, (a + 1) * LANES)
        xa, y = a // 4, a % 4
        queries = (q[0:TILE, cols], q[TILE : 2 * TILE, cols])
        for xb in range(2):
            n = (xa * 2 + xb) * 4 + y
            out[n, 0:64, :] = k[:, cols]
            out[n, 64:128, :] = v[:, cols]
            out[n, 128:192, :] = kz[:, cols]
            out[n, 192:256, :] = vz[:, cols]
            for t in range(2):
                out[n, 256 + 16 * t : 272 + 16 * t, :] = queries[t][16 * xb : 16 * xb + 16]


def attend_kernel(meta, slots, mine, twin, out, scores):
    xb, zh, c = meta[2], meta[4], meta[5]
    log_scale = math.log2(math.e) / math.sqrt(HEAD_DIM)
    refs = (mine, twin)
    groups = []
    for which in range(2):
        for other in range(2):
            zg = zh if other == 0 else 1 - zh
            cg = c if which == 0 else 1 - c
            groups.append((refs[which], other * 128, zg, cg))

    def place(src, zg, cg, late, u):
        device = src * 4 + zg * 2 + cg
        return (127 - device if late else device) * TILE + u

    def columns(late):
        col = lax.broadcasted_iota(jnp.int32, (1, 512), 1)
        return [place(col // TILE, zg, cg, late, col % TILE) for _, _, zg, cg in groups]

    def tiles(ref, low, count):
        return ref[:, low : low + count, :].reshape(16 * count, LANES)

    block = 128
    places = (columns(False), columns(True))
    for late in range(2):
        for part in range(256 // block):
            src0 = part * (block // 16)
            query = mine[src0 : src0 + block // 16, 256 + 16 * late : 272 + 16 * late, :]
            query = query.reshape(block, LANES)
            row = lax.broadcasted_iota(jnp.int32, (block, 1), 0)
            spot = place(src0 + row // 16, zh, c, bool(late), xb * 16 + row % 16)
            top = jnp.full((block, LANES), MASKED, F32)
            jobs = []
            for key_late in range(late + 1):
                for g, (ref, low, _, _) in enumerate(groups):
                    jobs.append((len(jobs), key_late, g, ref, low + TILE * key_late))
            for n, key_late, g, ref, low in jobs:
                keys = tiles(ref, low, TILE)
                found = lax.dot_general(
                    query, keys, (((1,), (1,)), ((), ())), preferred_element_type=F32
                )
                if key_late == late:
                    found = jnp.where(places[key_late][g] <= spot, found, MASKED)
                scores[:, n * 512 : (n + 1) * 512] = found
                for k in range(4):
                    top = jnp.maximum(top, found[:, k * LANES : (k + 1) * LANES])
            top = jnp.max(top, axis=1, keepdims=True)
            total = jnp.zeros((block, LANES), F32)
            summed = jnp.zeros((block, LANES), F32)
            for n, key_late, g, ref, low in jobs:
                weights = jnp.exp2((scores[:, n * 512 : (n + 1) * 512] - top) * log_scale)
                for k in range(4):
                    total = total + weights[:, k * LANES : (k + 1) * LANES]
                values = tiles(ref, low + 64, TILE)
                summed = summed + jnp.dot(
                    weights.astype(BF16), values, preferred_element_type=F32
                )
            result = (summed / jnp.sum(total, axis=1, keepdims=True)).astype(BF16)
            out[src0 : src0 + block // 16, 16 * late : 16 * late + 16, :] = result.reshape(
                block // 16, 16, LANES
            )

    def cache(n, carry):
        for slot in range(2):
            tile = slots[n * 2 + slot]
            held = jnp.maximum(tile, 0)
            late = (held >= 64).astype(jnp.int32)
            device = jnp.where(held >= 64, 127 - held, held)
            src = device // 4
            zd, cd = (device // 2) % 2, device % 2
            low = pl.multiple_of(jnp.where(zd == zh, 0, 128) + late * TILE, TILE)
            there = jnp.where(tile >= 0, 1, 0)
            near = jnp.where(cd == c, 1, 0)
            for kv in range(2):
                a = mine[src, pl.ds(pl.multiple_of(low + 64 * kv, TILE), TILE), :]
                b = twin[src, pl.ds(pl.multiple_of(low + 64 * kv, TILE), TILE), :]
                value = jnp.where(near == 1, a, b)
                value = jnp.where(there == 1, value, jnp.zeros_like(value))
                first = 32 + (slot * 2 + kv) * TILE
                out[n, first : first + TILE, :] = value
        return carry

    lax.fori_loop(0, 16, cache, 0)


def unpack_kernel(came, att, keys, values):
    for n in range(16):
        xa, xb, y = n // 8, (n // 4) % 2, n % 4
        a = xa * 4 + y
        cols = slice(a * LANES, (a + 1) * LANES)
        att[16 * xb : 16 * xb + 16, cols] = came[n, 0:16, :]
        att[TILE + 16 * xb : TILE + 16 * xb + 16, cols] = came[n, 16:32, :]
        for slot in range(2):
            rows = slice((xb * 2 + slot) * TILE, (xb * 2 + slot + 1) * TILE)
            low = 32 + slot * 2 * TILE
            keys[rows, cols] = came[n, low : low + TILE, :]
            values[rows, cols] = came[n, low + TILE : low + 2 * TILE, :]


def shape(dims, dtype=BF16):
    return jax.ShapeDtypeStruct(dims, dtype)


def body(stream, se_pre, se_post, se_taps, mr_pre, mr_post, mr_taps, query, key, value, owner):
    x, y, zh, c = (lax.axis_index(name) for name in CTX)
    me = ((x * 4 + y) * 2 + zh) * 2 + c
    meta = jnp.stack([me, x // 2, x % 2, y, zh, c, c, c]).astype(jnp.int32)
    rows, channels = stream.shape

    early_raw = jnp.concatenate([stream[24:32], se_pre[24:32]], axis=0)
    late_raw = jnp.concatenate([stream[56:64], se_pre[56:64]], axis=0)
    halo_early = ctx_route(early_raw, lambda i: i + 1)
    halo_late = ctx_route(late_raw, lambda i: i - 1)
    key_z = lax.ppermute(key, "zh", [(0, 1), (1, 0)])
    value_z = lax.ppermute(value, "zh", [(0, 1), (1, 0)])

    taps = jnp.pad(se_taps.T.astype(F32), ((0, 1), (0, 0)))
    sums = call(
        stats_kernel,
        shape((80, LANES), F32),
        [pltpu.VMEM((2, 40, channels), F32), pltpu.VMEM((rows, channels), F32), pltpu.VMEM((rows, channels), F32)],
        [S, V, V, V, V, V, V],
        flops=20_000_000,
        nbytes=900_000,
        name="stats",
    )(meta, stream, se_pre, se_post, taps, halo_early, halo_late)
    total = lax.psum(sums, "tp")
    mixed, early, late = call(
        mix_kernel,
        [shape((rows, channels)), shape((TILE, channels)), shape((TILE, channels))],
        [pltpu.VMEM((2, 40, LANES), F32), pltpu.VMEM((64, LANES), F32), pltpu.VMEM((2, 40, LANES), F32)],
        [S, V, V, V, V, V, V, V, V],
        flops=8_000_000,
        nbytes=1_500_000,
        name="mix",
    )(meta, stream, se_pre, se_post, taps, halo_early, halo_late, total, mr_pre)

    e2 = ctx_route(early, lambda i: i + 2)
    l2 = ctx_route(late, lambda i: i - 2)
    e4 = ctx_route(early, lambda i: i + 4)
    l4 = ctx_route(late, lambda i: i - 4)
    turn2 = ctx_route(early, lambda i: 125 - i if i > 61 else -1)
    turn4 = ctx_route(early, lambda i: 123 - i if i > 59 else -1)
    l2 = jnp.where(me >= 62, turn2, l2)
    l4 = jnp.where(me >= 60, turn4, l4)
    even = c == 0
    swap = jnp.stack(
        [
            jnp.where(even, early, e2),
            jnp.where(even, e2, e4),
            jnp.where(even, l2, late),
            jnp.where(even, l4, l2),
        ]
    )
    swapped = lax.ppermute(swap, "c", [(0, 1), (1, 0)])

    packed = call(pack_kernel, shape((16, 288, LANES)), (), [S] + [V] * 5, nbytes=3_000_000, name="pack")(
        meta, key, value, key_z, value_z, query
    )
    mine = lax.all_to_all(packed, ("x", "y"), 0, 0, tiled=True)
    twin = lax.ppermute(mine, "c", [(0, 1), (1, 0)])

    owners = owner[:, 0]
    tile_ids = jnp.arange(128, dtype=jnp.int32)
    earlier = tile_ids[:, None] > tile_ids[None, :]
    ranks = jnp.sum((earlier & (owners[:, None] == owners[None, :])).astype(jnp.int32), axis=1)
    place_of = owners * CAP + ranks
    want = (jnp.arange(16, dtype=jnp.int32)[:, None] * 4 + zh * 2 + c) * CAP
    want = (want + (x % 2) * 2 + jnp.arange(2, dtype=jnp.int32)[None, :]).reshape(32)
    match = want[:, None] == place_of[None, :]
    slots = jnp.sum(jnp.where(match, tile_ids[None, :] + 1, 0), axis=1) - 1

    answered = call(
        attend_kernel,
        shape((16, 160, LANES)),
        [pltpu.VMEM((128, 4096), F32)],
        [S, S, V, V],
        flops=1_000_000_000,
        nbytes=3_000_000,
        name="attend",
    )(meta, slots.astype(jnp.int32), mine, twin)
    came = lax.all_to_all(answered, ("x", "y"), 0, 0, tiled=True)
    attention_out, cache_keys, cache_values = call(
        unpack_kernel,
        [shape((rows, 1024)), shape((128, 1024)), shape((128, 1024))],
        (),
        [V],
        nbytes=1_300_000,
        name="unpack",
    )(came)
    decode_cache = jnp.stack([cache_keys, cache_values], axis=1)

    reversed_taps = jnp.pad(mr_taps[:, ::-1].astype(F32), ((0, 0), (1, 127)))
    hyena_stream, filter_state = call(
        conv_kernel,
        [shape((rows, channels)), shape((128, channels))],
        [pltpu.VMEM((2, 160, channels), BF16)],
        [S] + [V] * 10,
        flops=100_000_000,
        nbytes=3_000_000,
        name="conv",
    )(meta, reversed_taps, mixed, mr_post, early, late, e2, e4, l2, l4, swapped)
    return hyena_stream, attention_out, decode_cache, filter_state


def solution(mesh):
    fine = Mesh(mesh.devices.reshape(4, 4, 2, 2, 4), (*CTX, "tp"))
    block = P(CTX, "tp")
    in_specs = (block, block, block, P("tp", None), block, block, P("tp", None), block, block, block, P())
    out_specs = (block, block, P(CTX, None, "tp"), block)
    return jax.shard_map(body, mesh=fine, in_specs=in_specs, out_specs=out_specs, check_vma=False)
```

```python
import functools
import math

import jax
import jax.numpy as jnp
from jax import lax
from jax.experimental import pallas as pl
from jax.experimental.pallas import tpu as pltpu
from jax.sharding import Mesh, PartitionSpec as P

HEAD_DIM = 128
CAP = 4
EPS_NORM = 1e-06
MASKED = -1e30
CTX = ("x", "y", "zh", "c")
F32 = jnp.float32
BF16 = jnp.bfloat16
LANES = 128
TILE = 32
TAPS = 7
HALO = 40
PAIRS = tuple((a, b) for a in range(TAPS + 1) for b in range(a, TAPS + 1))


def ctx_route(array, target):
    pairs = [(i, target(i)) for i in range(64) if 0 <= target(i) < 64]
    return lax.ppermute(array, CTX, pairs)


def next_chip(i):
    return 63 if i == 63 else (i + 1 if i % 2 else i - 1)


def across(i):
    return (i + 1 if i % 2 else i - 1) % 64


def second_chip(i):
    return {63: 61, 61: 63}.get(i, i + 3 if i % 2 else i - 3)


SWAP = [(0, 1), (1, 0)]


def call(kernel, out_shape, scratch=(), in_spaces=None, flops=0, nbytes=0, name=None, out_space=pltpu.VMEM, vmem=24):
    specs = [pl.BlockSpec(memory_space=space) for space in in_spaces]
    if isinstance(out_shape, (list, tuple)):
        outs = [pl.BlockSpec(memory_space=pltpu.VMEM) for _ in out_shape]
    else:
        outs = pl.BlockSpec(memory_space=out_space)
    return pl.pallas_call(
        kernel,
        out_shape=out_shape,
        in_specs=specs,
        out_specs=outs,
        scratch_shapes=list(scratch),
        compiler_params=pltpu.CompilerParams(vmem_limit_bytes=vmem * 1024 * 1024),
        cost_estimate=pl.CostEstimate(flops=flops, bytes_accessed=nbytes, transcendentals=0),
        name=name,
    )


V, S = pltpu.VMEM, pltpu.SMEM


def lanes_at(index, width):
    return pl.ds(pl.multiple_of(index * width, width), width)


def halo_rows(meta, far, near, early, step):
    odd = meta[5] == 1
    rows = pl.ds(pl.multiple_of(128 + step // 8 * 16, 16), 16)
    other = far[rows, lanes_at(step % 8, LANES)].astype(F32)
    other = jnp.where(meta[0] == 0, jnp.zeros_like(other), other)
    twin = near[:, lanes_at(step, LANES)].astype(F32)
    before = jnp.where(odd, twin, other)
    after = jnp.where(meta[0] == 63, early, jnp.where(odd, other, twin))
    return before, after


def sum_pairs(out, row, base, tiles, terms_of, packed=None):
    zero = jnp.zeros((8, LANES), F32)
    lane = lax.broadcasted_iota(jnp.int32, (8, LANES), 1)
    packed = zero if packed is None else packed
    for tile in range(tiles):

        def collect(step, sums, tile=tile):
            terms = terms_of(tile, lanes_at(step, LANES))
            return tuple(t + terms[a] * terms[b] for t, (a, b) in zip(sums, PAIRS))

        sums = lax.fori_loop(0, base, collect, (zero,) * len(PAIRS), unroll=4)
        for q, part in enumerate(sums):
            packed = jnp.where(lane == q + 64 * tile, jnp.sum(part, axis=1, keepdims=True), packed)
    out[row : row + 8, :] = packed


def stats_kernel(stream, pre, post, taps, out, us, sf, pf, tf):
    tf[0:TAPS, :] = taps[...].astype(F32)
    chunks = stream.shape[1] // LANES

    def prepare(step, carry):
        cs = lanes_at(step, LANES)
        s = stream[:, cs].astype(F32)
        sf[:, cs] = s
        pf[:, cs] = post[:, cs].astype(F32)
        us[:, cs] = s * pre[:, cs].astype(F32)
        return carry

    lax.fori_loop(0, chunks, prepare, 0, unroll=2)
    out[0:8, :] = jnp.zeros((8, LANES), F32)
    for group in range(1, TILE // 8):

        def terms_of(tile, cs, group=group):
            row = tile * TILE + group * 8
            gate = pf[row : row + 8, cs]
            behind = [us[pl.ds(row - j, 8), cs] for j in range(TAPS)]
            return [sf[row : row + 8, cs]] + [tf[j : j + 1, cs] * gate * behind[j] for j in range(TAPS)]

        sum_pairs(out, group * 8, chunks, 2, terms_of)


def head_kernel(meta, stream, pre, post, taps, far, near, partial, out, us, sf, pf, tf):
    tf[0:TAPS, :] = taps[...].astype(F32)
    chunks = stream.shape[1] // LANES

    def prepare(step, carry):
        cs = lanes_at(step, LANES)
        own = [ref[16:TILE, cs].astype(F32)[8:16] for ref in (stream, pre)]
        halos = halo_rows(meta, far, near, jnp.concatenate(own, axis=0), step)
        squares = []
        for tile in range(2):
            halo = halos[tile]
            rows = slice(tile * TILE, tile * TILE + 16)
            s = stream[rows, cs].astype(F32)[0:8]
            sf[tile, :, cs] = s
            pf[tile, :, cs] = post[rows, cs].astype(F32)[0:8]
            us[tile, 0:8, cs] = halo[0:8] * halo[8:16]
            us[tile, 8:16, cs] = s * pre[rows, cs].astype(F32)[0:8]
            squares.append(carry[tile] + halo[0:8] * halo[0:8])
        return tuple(squares)

    zero = jnp.zeros((8, LANES), F32)
    squares = lax.fori_loop(0, chunks, prepare, (zero, zero), unroll=2)
    lane = lax.broadcasted_iota(jnp.int32, (8, LANES), 1)
    packed = zero
    for tile in range(2):
        packed = jnp.where(lane == HALO + 64 * tile, jnp.sum(squares[tile], axis=1, keepdims=True), packed)

    def terms_of(tile, cs):
        gate = pf[tile, :, cs]
        behind = [us[tile, pl.ds(8 - j, 8), cs] for j in range(TAPS)]
        return [sf[tile, :, cs]] + [tf[j : j + 1, cs] * gate * behind[j] for j in range(TAPS)]

    sum_pairs(out, 0, chunks, 2, terms_of, packed)
    out[8:TILE, :] = partial[8:TILE, :]


def pack_kernel(k, v, far, q, out):
    for a in range(8):
        cols = slice(a * LANES, (a + 1) * LANES)
        for xb in range(2):
            n = ((a // 4) * 2 + xb) * 4 + a % 4
            out[n, 0:64, :] = k[:, cols]
            out[n, 64:128, :] = v[:, cols]
            out[n, 128:256, :] = far[0:128, cols]
            for t in range(2):
                low = TILE * t + 16 * xb
                out[n, 256 + 16 * t : 272 + 16 * t, :] = q[low : low + 16, cols]


def mix_kernel(
    meta, stream, pre, post, mrpre, taps, he, hl, half, other, mixed, keep, give,
    sc, s2, xs, tf,
):
    odd = meta[5] == 1
    tf[0:TAPS, :] = taps[...].astype(F32)
    width = 1.0 / 8192.0
    total = half[...] + other[...]
    scale = lax.rsqrt(total * width + EPS_NORM)
    for tile in range(2):
        near = 64 * tile
        far = near + HALO
        sc[tile, 0:8, :] = jnp.broadcast_to(scale[0:8, far : far + 1], (8, LANES))
        sc[tile, 8:40, :] = jnp.broadcast_to(scale[:, near : near + 1], (TILE, LANES))
    lane = lax.broadcasted_iota(jnp.int32, (TILE, LANES), 1)
    for tile in range(2):
        factor = [jnp.ones((TILE, LANES), F32)]
        for j in range(TAPS):
            factor.append(sc[tile, pl.ds(8 - j, TILE), :])
        weight = jnp.zeros((TILE, LANES), F32)
        for q, (a, b) in enumerate(PAIRS):
            term = factor[a] * factor[b]
            weight = jnp.where(lane == q + 64 * tile, term if a == b else term * 2.0, weight)
        rows = slice(tile * TILE, (tile + 1) * TILE)
        squares = jnp.sum(weight * total, axis=1, keepdims=True)
        second = lax.rsqrt(jnp.maximum(squares, 0.0) * width + EPS_NORM)
        s2[rows, :] = jnp.broadcast_to(second, (TILE, LANES))

    def one(step, carry):
        cs = lanes_at(step, LANES)
        s = stream[:, cs].astype(F32)
        p = pre[:, cs].astype(F32)
        u = s * p
        own = jnp.concatenate([s[TILE - 8 : TILE], p[TILE - 8 : TILE]], axis=0)
        before, after = halo_rows(meta, he, hl, own, step)
        eu, lu = before[0:8] * before[8:16], after[0:8] * after[8:16]
        gate = post[:, cs].astype(F32)
        front = mrpre[:, cs].astype(F32)
        for tile, halo in enumerate((eu, lu)):
            rows = slice(tile * TILE, (tile + 1) * TILE)
            xs[tile, 0:8, :] = (halo * sc[tile, 0:8, :]).astype(BF16).astype(F32)
            xs[tile, 8:40, :] = (u[rows] * sc[tile, 8:40, :]).astype(BF16).astype(F32)
        values = []
        for tile in range(2):
            rows = slice(tile * TILE, (tile + 1) * TILE)
            acc = jnp.zeros((TILE, LANES), F32)
            for j in range(TAPS):
                acc = acc + tf[j : j + 1, cs] * xs[tile, pl.ds(8 - j, TILE), :]
            value = (s[rows] + gate[rows] * acc).astype(BF16)
            mixed[rows, cs] = value
            values.append((front[rows] * value.astype(F32) * s2[rows, :]).astype(BF16))
        keep[:, cs] = jnp.where(odd, values[0], values[1])
        give[:, cs] = jnp.where(odd, values[1], values[0])
        return carry

    lax.fori_loop(0, stream.shape[1] // LANES, one, 0)


def conv_kernel(meta, taps, mixed, post, keep, give, got, one, two, rest, out, state, ext):
    ext[0, 0:32, :] = two[32:64, :]
    ext[0, 32:64, :] = two[0:32, :]
    ext[0, 64:96, :] = one[32:64, :]
    ext[0, 96:128, :] = one[0:32, :]
    ext[0, 128:160, :] = give[...]
    ext[1, 0:32, :] = rest[64:96, :]
    ext[1, 32:64, :] = rest[32:64, :]
    ext[1, 64:96, :] = rest[0:32, :]
    ext[1, 96:128, :] = got[...]
    ext[1, 128:160, :] = keep[...]
    group_width = out.shape[1] // taps.shape[0]
    for g in range(taps.shape[0]):
        row = jnp.broadcast_to(taps[g : g + 1, :], (TILE, 256))
        toeplitz = pltpu.roll(row, 0, 1, stride=1, stride_axis=0)[:, 0:160].astype(BF16)
        cols = slice(g * group_width, (g + 1) * group_width)
        for part in range(2):
            place = meta[5] if part == 0 else 1 - meta[5]
            rows = pl.ds(pl.multiple_of(place * TILE, TILE), TILE)
            acc = jnp.dot(toeplitz, ext[part, :, cols], preferred_element_type=F32)
            value = mixed[rows, cols].astype(F32) + post[rows, cols].astype(F32) * acc
            out[rows, cols] = value.astype(BF16)

    @pl.when(meta[0] == 0)
    def _():
        state[...] = ext[1, 32:160, :]

    @pl.when(meta[0] != 0)
    def _():
        state[...] = jnp.zeros_like(state)


def attend_kernel(meta, slots, mine, twin, after, out, scores):
    xb, zh, c = meta[2], meta[4], meta[5]

    def pieces(n, carry):
        for slot in range(2):
            tile = slots[n * 2 + slot]
            held = jnp.maximum(tile, 0)
            late = (held >= 64).astype(jnp.int32)
            device = jnp.where(held >= 64, 127 - held, held)
            across_z = (device // 2) % 2 != zh
            holder = jnp.where(device % 2 == 1, device + 1, device + 63) % 64
            holder = jnp.where(across_z, holder, device)
            src, cd = holder // 4, holder % 2
            low = jnp.where(across_z, 128, 0) + late * TILE
            for kv in range(2):
                rows = pl.ds(pl.multiple_of(low + 64 * kv, TILE), TILE)
                value = jnp.where(cd == c, mine[src, rows, :], twin[src, rows, :])
                value = jnp.where(tile >= 0, value, jnp.zeros_like(value))
                first = 32 + (slot * 2 + kv) * TILE
                out[n, first : first + TILE, :] = value
        return carry

    lax.fori_loop(0, 16, pieces, 0, unroll=4)
    log_scale = math.log2(math.e) / math.sqrt(HEAD_DIM)
    def owner(core, far):
        def of(src):
            device = src * 4 + zh * 2 + core
            return (jnp.where(core == 1, device + 1, device + 63) % 64) if far else device

        return of

    groups = [(ref, 128 * far, owner(core, far)) for ref, core in ((mine, c), (twin, 1 - c)) for far in range(2)]

    def place(device, late, u):
        return (127 - device if late else device) * TILE + u

    def columns(late):
        col = lax.broadcasted_iota(jnp.int32, (1, 512), 1)
        return [place(of(col // TILE), late, col % TILE) for _, _, of in groups]

    def tiles(ref, low, count):
        return ref[:, low : low + count, :].reshape(16 * count, LANES)

    block = 128
    places = (columns(False), columns(True))
    for late in range(2):
        for part in range(256 // block):
            src0 = part * (block // 16)
            query = mine[src0 : src0 + block // 16, 256 + 16 * late : 272 + 16 * late, :]
            query = query.reshape(block, LANES)
            row = lax.broadcasted_iota(jnp.int32, (block, 1), 0)
            spot = place((src0 + row // 16) * 4 + zh * 2 + c, bool(late), xb * 16 + row % 16)
            top = jnp.full((block, LANES), MASKED, F32)
            jobs = []
            for key_late in range(late + 1):
                for g, (ref, low, _) in enumerate(groups):
                    jobs.append((len(jobs), key_late, g, ref, low + TILE * key_late))
            for n, key_late, g, ref, low in jobs:
                keys = tiles(ref, low, TILE)
                found = lax.dot_general(
                    query, keys, (((1,), (1,)), ((), ())), preferred_element_type=F32
                )
                if key_late == late:
                    found = jnp.where(places[key_late][g] <= spot, found, MASKED)
                scores[:, n * 512 : (n + 1) * 512] = found
                for k in range(4):
                    top = jnp.maximum(top, found[:, k * LANES : (k + 1) * LANES])
            top = jnp.max(top, axis=1, keepdims=True)
            total = jnp.zeros((block, LANES), F32)
            summed = jnp.zeros((block, LANES), F32)
            for n, key_late, g, ref, low in jobs:
                weights = jnp.exp2((scores[:, n * 512 : (n + 1) * 512] - top) * log_scale)
                for k in range(4):
                    total = total + weights[:, k * LANES : (k + 1) * LANES]
                values = tiles(ref, low + 64, TILE)
                summed = summed + jnp.dot(
                    weights.astype(BF16), values, preferred_element_type=F32
                )
            result = (summed / jnp.sum(total, axis=1, keepdims=True)).astype(BF16)
            out[src0 : src0 + block // 16, 16 * late : 16 * late + 16, :] = result.reshape(
                block // 16, 16, LANES
            )


def unpack_kernel(came, att, keys, values):
    for n in range(16):
        xa, xb, y = n // 8, (n // 4) % 2, n % 4
        a = xa * 4 + y
        cols = slice(a * LANES, (a + 1) * LANES)
        att[16 * xb : 16 * xb + 16, cols] = came[n, 0:16, :]
        att[TILE + 16 * xb : TILE + 16 * xb + 16, cols] = came[n, 16:32, :]
        for slot in range(2):
            rows = slice((xb * 2 + slot) * TILE, (xb * 2 + slot + 1) * TILE)
            low = 32 + slot * 2 * TILE
            keys[rows, cols] = came[n, low : low + TILE, :]
            values[rows, cols] = came[n, low + TILE : low + 2 * TILE, :]


def shape(dims, dtype=BF16):
    return jax.ShapeDtypeStruct(dims, dtype)


def body(stream, se_pre, se_post, se_taps, mr_pre, mr_post, mr_taps, query, key, value, owner):
    x, y, zh, c = (lax.axis_index(name) for name in CTX)
    me = ((x * 4 + y) * 2 + zh) * 2 + c
    meta = jnp.stack([me, x // 2, x % 2, y, zh, c, c, c]).astype(jnp.int32)
    rows, channels = stream.shape

    odd = c == 1
    early_raw = jnp.concatenate([stream[24:32], se_pre[24:32]], axis=0)
    late_raw = jnp.concatenate([stream[56:64], se_pre[56:64]], axis=0)
    outer = jnp.where(odd, early_raw, late_raw)
    halo_near = lax.ppermute(jnp.where(odd, late_raw, early_raw), "c", SWAP)
    crossing = jnp.concatenate([key, value, outer[:, :1024], outer[:, 1024:]], axis=0)
    far = ctx_route(crossing, across)
    taps = se_taps.T
    partial = call(
        stats_kernel,
        shape((TILE, LANES), F32),
        [pltpu.VMEM((rows, channels), F32)] * 3 + [pltpu.VMEM((8, channels), F32)],
        [V] * 4,
        flops=15_000_000,
        nbytes=800_000,
        name="stats",
    )(stream, se_pre, se_post, taps)
    sums = call(
        head_kernel,
        shape((TILE, LANES), F32),
        [pltpu.VMEM((2, 16, channels), F32)] + [pltpu.VMEM((2, 8, channels), F32)] * 2 + [pltpu.VMEM((8, channels), F32)],
        [S] + [V] * 7,
        flops=5_000_000,
        nbytes=300_000,
        name="head",
    )(meta, stream, se_pre, se_post, taps, far, halo_near, partial)
    packed, sums = lax.optimization_barrier((far, sums))
    half = sums + lax.ppermute(sums, "tp", [(i, i ^ 1) for i in range(4)])
    other = lax.ppermute(half, "tp", [(i, i ^ 2) for i in range(4)])
    mixed, keep, give = call(
        mix_kernel,
        [shape((rows, channels)), shape((TILE, channels)), shape((TILE, channels))],
        [pltpu.VMEM((2, 40, LANES), F32), pltpu.VMEM((64, LANES), F32), pltpu.VMEM((2, 40, LANES), F32)]
        + [pltpu.VMEM((8, channels), F32)],
        [S] + [V] * 9,
        flops=8_000_000,
        nbytes=3_500_000,
        name="mix",
    )(meta, stream, se_pre, se_post, mr_pre, taps, far, halo_near, half, other)

    got = lax.ppermute(give, "c", SWAP)
    pair = jnp.concatenate([keep, got], axis=0)
    heads = call(
        pack_kernel, shape((16, 288, LANES)), (), [V] * 4, nbytes=2_000_000, name="pack"
    )(key, value, packed, query)
    mine = lax.all_to_all(heads, ("x", "y"), 0, 0, tiled=True)
    two = ctx_route(pair, second_chip)
    one = ctx_route(pair, next_chip)
    mark = pair[:16, :128]
    mine, pair = lax.optimization_barrier((mine, pair))
    share = jnp.concatenate([one, two[:TILE]], axis=0)

    rest = lax.ppermute(share, "c", SWAP)
    twin = lax.ppermute(mine, "c", [(0, 1), (1, 0)])

    owners = owner[:, 0]
    tile_ids = jnp.arange(128, dtype=jnp.int32)
    earlier = tile_ids[:, None] > tile_ids[None, :]
    ranks = jnp.sum((earlier & (owners[:, None] == owners[None, :])).astype(jnp.int32), axis=1)
    place_of = owners * CAP + ranks
    want = (jnp.arange(16, dtype=jnp.int32)[:, None] * 4 + zh * 2 + c) * CAP
    want = (want + (x % 2) * 2 + jnp.arange(2, dtype=jnp.int32)[None, :]).reshape(32)
    match = want[:, None] == place_of[None, :]
    slots = jnp.sum(jnp.where(match, tile_ids[None, :] + 1, 0), axis=1) - 1

    answered = call(
        attend_kernel,
        shape((16, 160, LANES)),
        [pltpu.VMEM((128, 4096), F32)],
        [S, S, V, V, V],
        flops=1_000_000_000,
        nbytes=3_000_000,
        name="attend",
    )(meta, slots.astype(jnp.int32), mine, twin, mark)
    came = lax.all_to_all(answered, ("x", "y"), 0, 0, tiled=True)
    attention_out, cache_keys, cache_values = call(
        unpack_kernel,
        [shape((rows, 1024)), shape((128, 1024)), shape((128, 1024))],
        (),
        [V],
        nbytes=1_300_000,
        name="unpack",
    )(came)
    decode_cache = jnp.stack([cache_keys, cache_values], axis=1)

    reversed_taps = jnp.pad(mr_taps[:, ::-1].astype(F32), ((0, 0), (1, 127)))
    hyena_stream, filter_state = call(
        conv_kernel,
        [shape((rows, channels)), shape((128, channels))],
        [pltpu.VMEM((2, 160, channels), BF16)],
        [S] + [V] * 9,
        flops=100_000_000,
        nbytes=3_000_000,
        name="conv",
    )(meta, reversed_taps, mixed, mr_post, keep, give, got, one, two, rest)
    return hyena_stream, attention_out, decode_cache, filter_state


def solution(mesh):
    fine = Mesh(mesh.devices.reshape(4, 4, 2, 2, 4), (*CTX, "tp"))
    block = P(CTX, "tp")
    in_specs = (block, block, block, P("tp", None), block, block, P("tp", None), block, block, block, P())
    out_specs = (block, block, P(CTX, None, "tp"), block)
    return jax.shard_map(body, mesh=fine, in_specs=in_specs, out_specs=out_specs, check_vma=False)
```

```python
import functools
import math

import jax
import jax.numpy as jnp
from jax import lax
from jax.experimental import pallas as pl
from jax.experimental.pallas import tpu as pltpu
from jax.sharding import Mesh, PartitionSpec as P

HEAD_DIM = 128
CAP = 4
EPS_NORM = 1e-06
MASKED = -1e30
CTX = ("x", "y", "zh", "c")
F32 = jnp.float32
BF16 = jnp.bfloat16
LANES = 128
TILE = 32
TAPS = 7
HALO = 40
PAIRS = tuple((a, b) for a in range(TAPS + 1) for b in range(a, TAPS + 1))


def ctx_route(array, target):
    pairs = [(i, target(i)) for i in range(64) if 0 <= target(i) < 64]
    return lax.ppermute(array, CTX, pairs)


def next_chip(i):
    return 63 if i == 63 else (i + 1 if i % 2 else i - 1)


def across(i):
    return (i + 1 if i % 2 else i - 1) % 64


def second_chip(i):
    return {63: 61, 61: 63}.get(i, i + 3 if i % 2 else i - 3)


SWAP = [(0, 1), (1, 0)]


def call(kernel, out_shape, scratch=(), in_spaces=None, flops=0, nbytes=0, name=None, out_space=pltpu.VMEM, vmem=24):
    specs = [pl.BlockSpec(memory_space=space) for space in in_spaces]
    if isinstance(out_shape, (list, tuple)):
        outs = [pl.BlockSpec(memory_space=pltpu.VMEM) for _ in out_shape]
    else:
        outs = pl.BlockSpec(memory_space=out_space)
    return pl.pallas_call(
        kernel,
        out_shape=out_shape,
        in_specs=specs,
        out_specs=outs,
        scratch_shapes=list(scratch),
        compiler_params=pltpu.CompilerParams(vmem_limit_bytes=vmem * 1024 * 1024),
        cost_estimate=pl.CostEstimate(flops=flops, bytes_accessed=nbytes, transcendentals=0),
        name=name,
    )


V, S = pltpu.VMEM, pltpu.SMEM


def lanes_at(index, width):
    return pl.ds(pl.multiple_of(index * width, width), width)


def halo_rows(meta, far, near, early, step):
    odd = meta[5] == 1
    rows = pl.ds(pl.multiple_of(64 + step // 8 * 16, 16), 16)
    other = far[rows, lanes_at(step % 8, LANES)].astype(F32)
    other = jnp.where(meta[0] == 0, jnp.zeros_like(other), other)
    twin = near[:, lanes_at(step, LANES)].astype(F32)
    before = jnp.where(odd, twin, other)
    after = jnp.where(meta[0] == 63, early, jnp.where(odd, other, twin))
    return before, after


def sum_pairs(out, row, base, tiles, terms_of, packed=None):
    zero = jnp.zeros((8, LANES), F32)
    lane = lax.broadcasted_iota(jnp.int32, (8, LANES), 1)
    packed = zero if packed is None else packed
    for tile in range(tiles):

        def collect(step, sums, tile=tile):
            terms = terms_of(tile, lanes_at(step, LANES))
            return tuple(t + terms[a] * terms[b] for t, (a, b) in zip(sums, PAIRS))

        sums = lax.fori_loop(0, base, collect, (zero,) * len(PAIRS), unroll=4)
        for q, part in enumerate(sums):
            packed = jnp.where(lane == q + 64 * tile, jnp.sum(part, axis=1, keepdims=True), packed)
    out[row : row + 8, :] = packed


def stats_kernel(stream, pre, post, taps, out, us, sf, pf, tf):
    tf[0:TAPS, :] = taps[...].astype(F32)
    chunks = stream.shape[1] // LANES

    def prepare(step, carry):
        cs = lanes_at(step, LANES)
        s = stream[:, cs].astype(F32)
        sf[:, cs] = s
        pf[:, cs] = post[:, cs].astype(F32)
        us[:, cs] = s * pre[:, cs].astype(F32)
        return carry

    lax.fori_loop(0, chunks, prepare, 0, unroll=2)
    out[0:8, :] = jnp.zeros((8, LANES), F32)
    for group in range(1, TILE // 8):

        def terms_of(tile, cs, group=group):
            row = tile * TILE + group * 8
            gate = pf[row : row + 8, cs]
            behind = [us[pl.ds(row - j, 8), cs] for j in range(TAPS)]
            return [sf[row : row + 8, cs]] + [tf[j : j + 1, cs] * gate * behind[j] for j in range(TAPS)]

        sum_pairs(out, group * 8, chunks, 2, terms_of)


def head_kernel(meta, stream, pre, post, taps, far, near, partial, out, us, sf, pf, tf):
    tf[0:TAPS, :] = taps[...].astype(F32)
    chunks = stream.shape[1] // LANES

    def prepare(step, carry):
        cs = lanes_at(step, LANES)
        own = [ref[16:TILE, cs].astype(F32)[8:16] for ref in (stream, pre)]
        halos = halo_rows(meta, far, near, jnp.concatenate(own, axis=0), step)
        squares = []
        for tile in range(2):
            halo = halos[tile]
            rows = slice(tile * TILE, tile * TILE + 16)
            s = stream[rows, cs].astype(F32)[0:8]
            sf[tile, :, cs] = s
            pf[tile, :, cs] = post[rows, cs].astype(F32)[0:8]
            us[tile, 0:8, cs] = halo[0:8] * halo[8:16]
            us[tile, 8:16, cs] = s * pre[rows, cs].astype(F32)[0:8]
            squares.append(carry[tile] + halo[0:8] * halo[0:8])
        return tuple(squares)

    zero = jnp.zeros((8, LANES), F32)
    squares = lax.fori_loop(0, chunks, prepare, (zero, zero), unroll=2)
    lane = lax.broadcasted_iota(jnp.int32, (8, LANES), 1)
    packed = zero
    for tile in range(2):
        packed = jnp.where(lane == HALO + 64 * tile, jnp.sum(squares[tile], axis=1, keepdims=True), packed)

    def terms_of(tile, cs):
        gate = pf[tile, :, cs]
        behind = [us[tile, pl.ds(8 - j, 8), cs] for j in range(TAPS)]
        return [sf[tile, :, cs]] + [tf[j : j + 1, cs] * gate * behind[j] for j in range(TAPS)]

    sum_pairs(out, 0, chunks, 2, terms_of, packed)
    out[8:TILE, :] = partial[8:TILE, :]


def pack_kernel(k, v, far, far_values, q, out):
    for a in range(8):
        cols = slice(a * LANES, (a + 1) * LANES)
        for xb in range(2):
            n = ((a // 4) * 2 + xb) * 4 + a % 4
            out[n, 0:64, :] = k[:, cols]
            out[n, 64:128, :] = v[:, cols]
            out[n, 128:192, :] = far[0:64, cols]
            out[n, 192:256, :] = far_values[:, cols]
            for t in range(2):
                low = TILE * t + 16 * xb
                out[n, 256 + 16 * t : 272 + 16 * t, :] = q[low : low + 16, cols]


def mix_kernel(
    meta, stream, pre, post, mrpre, taps, he, hl, half, other, mixed, keep, give,
    sc, s2, xs, tf,
):
    odd = meta[5] == 1
    tf[0:TAPS, :] = taps[...].astype(F32)
    width = 1.0 / 8192.0
    total = half[...] + other[...]
    scale = lax.rsqrt(total * width + EPS_NORM)
    for tile in range(2):
        near = 64 * tile
        far = near + HALO
        sc[tile, 0:8, :] = jnp.broadcast_to(scale[0:8, far : far + 1], (8, LANES))
        sc[tile, 8:40, :] = jnp.broadcast_to(scale[:, near : near + 1], (TILE, LANES))
    lane = lax.broadcasted_iota(jnp.int32, (TILE, LANES), 1)
    for tile in range(2):
        factor = [jnp.ones((TILE, LANES), F32)]
        for j in range(TAPS):
            factor.append(sc[tile, pl.ds(8 - j, TILE), :])
        weight = jnp.zeros((TILE, LANES), F32)
        for q, (a, b) in enumerate(PAIRS):
            term = factor[a] * factor[b]
            weight = jnp.where(lane == q + 64 * tile, term if a == b else term * 2.0, weight)
        rows = slice(tile * TILE, (tile + 1) * TILE)
        squares = jnp.sum(weight * total, axis=1, keepdims=True)
        second = lax.rsqrt(jnp.maximum(squares, 0.0) * width + EPS_NORM)
        s2[rows, :] = jnp.broadcast_to(second, (TILE, LANES))

    def one(step, carry):
        cs = lanes_at(step, LANES)
        s = stream[:, cs].astype(F32)
        p = pre[:, cs].astype(F32)
        u = s * p
        own = jnp.concatenate([s[TILE - 8 : TILE], p[TILE - 8 : TILE]], axis=0)
        before, after = halo_rows(meta, he, hl, own, step)
        eu, lu = before[0:8] * before[8:16], after[0:8] * after[8:16]
        gate = post[:, cs].astype(F32)
        front = mrpre[:, cs].astype(F32)
        for tile, halo in enumerate((eu, lu)):
            rows = slice(tile * TILE, (tile + 1) * TILE)
            xs[tile, 0:8, :] = (halo * sc[tile, 0:8, :]).astype(BF16).astype(F32)
            xs[tile, 8:40, :] = (u[rows] * sc[tile, 8:40, :]).astype(BF16).astype(F32)
        values = []
        for tile in range(2):
            rows = slice(tile * TILE, (tile + 1) * TILE)
            acc = jnp.zeros((TILE, LANES), F32)
            for j in range(TAPS):
                acc = acc + tf[j : j + 1, cs] * xs[tile, pl.ds(8 - j, TILE), :]
            value = (s[rows] + gate[rows] * acc).astype(BF16)
            mixed[rows, cs] = value
            values.append((front[rows] * value.astype(F32) * s2[rows, :]).astype(BF16))
        keep[:, cs] = jnp.where(odd, values[0], values[1])
        give[:, cs] = jnp.where(odd, values[1], values[0])
        return carry

    lax.fori_loop(0, stream.shape[1] // LANES, one, 0)


def conv_kernel(meta, taps, mixed, post, keep, give, got, one, two, rest, out, state, ext):
    ext[0, 0:32, :] = two[32:64, :]
    ext[0, 32:64, :] = two[0:32, :]
    ext[0, 64:96, :] = one[32:64, :]
    ext[0, 96:128, :] = one[0:32, :]
    ext[0, 128:160, :] = give[...]
    ext[1, 0:32, :] = rest[64:96, :]
    ext[1, 32:64, :] = rest[32:64, :]
    ext[1, 64:96, :] = rest[0:32, :]
    ext[1, 96:128, :] = got[...]
    ext[1, 128:160, :] = keep[...]
    group_width = out.shape[1] // taps.shape[0]
    for g in range(taps.shape[0]):
        row = jnp.broadcast_to(taps[g : g + 1, :], (TILE, 256))
        toeplitz = pltpu.roll(row, 0, 1, stride=1, stride_axis=0)[:, 0:160].astype(BF16)
        cols = slice(g * group_width, (g + 1) * group_width)
        for part in range(2):
            place = meta[5] if part == 0 else 1 - meta[5]
            rows = pl.ds(pl.multiple_of(place * TILE, TILE), TILE)
            acc = jnp.dot(toeplitz, ext[part, :, cols], preferred_element_type=F32)
            value = mixed[rows, cols].astype(F32) + post[rows, cols].astype(F32) * acc
            out[rows, cols] = value.astype(BF16)

    @pl.when(meta[0] == 0)
    def _():
        state[...] = ext[1, 32:160, :]

    @pl.when(meta[0] != 0)
    def _():
        state[...] = jnp.zeros_like(state)


def slots_kernel(meta, owner_row, owner_col, out):
    xb, zh, c = meta[2], meta[4], meta[5]
    row = lax.broadcasted_iota(jnp.int32, (128, 128), 0)
    col = lax.broadcasted_iota(jnp.int32, (128, 128), 1)
    mine = owner_col[...]
    before = (owner_row[...] == mine) & (col < row)
    rank = jnp.sum(jnp.where(before, 1, 0), axis=1, keepdims=True)
    want = (col // 2 * 4 + zh * 2 + c) * CAP + xb * 2 + col % 2
    found = (mine * CAP + rank == want) & (col < 32)
    out[...] = jnp.sum(jnp.where(found, row + 1, 0), axis=0, keepdims=True) - 1


def attend_kernel(meta, slots, mine, twin, after, out, scores):
    xb, zh, c = meta[2], meta[4], meta[5]

    def pieces(n, carry):
        for slot in range(2):
            tile = slots[0, n * 2 + slot]
            held = jnp.maximum(tile, 0)
            late = (held >= 64).astype(jnp.int32)
            device = jnp.where(held >= 64, 127 - held, held)
            across_z = (device // 2) % 2 != zh
            holder = jnp.where(device % 2 == 1, device + 1, device + 63) % 64
            holder = jnp.where(across_z, holder, device)
            src, cd = holder // 4, holder % 2
            low = jnp.where(across_z, 128, 0) + late * TILE
            for kv in range(2):
                rows = pl.ds(pl.multiple_of(low + 64 * kv, TILE), TILE)
                value = jnp.where(cd == c, mine[src, rows, :], twin[src, rows, :])
                value = jnp.where(tile >= 0, value, jnp.zeros_like(value))
                first = 32 + (slot * 2 + kv) * TILE
                out[n, first : first + TILE, :] = value
        return carry

    lax.fori_loop(0, 16, pieces, 0, unroll=4)
    log_scale = math.log2(math.e) / math.sqrt(HEAD_DIM)
    def owner(core, far):
        def of(src):
            device = src * 4 + zh * 2 + core
            return (jnp.where(core == 1, device + 1, device + 63) % 64) if far else device

        return of

    groups = [(ref, 128 * far, owner(core, far)) for ref, core in ((mine, c), (twin, 1 - c)) for far in range(2)]

    def place(device, late, u):
        return (127 - device if late else device) * TILE + u

    def columns(late):
        col = lax.broadcasted_iota(jnp.int32, (1, 512), 1)
        return [place(of(col // TILE), late, col % TILE) for _, _, of in groups]

    def tiles(ref, low, count):
        return ref[:, low : low + count, :].reshape(16 * count, LANES)

    block = 128
    places = (columns(False), columns(True))
    for late in range(2):
        for part in range(256 // block):
            src0 = part * (block // 16)
            query = mine[src0 : src0 + block // 16, 256 + 16 * late : 272 + 16 * late, :]
            query = query.reshape(block, LANES)
            row = lax.broadcasted_iota(jnp.int32, (block, 1), 0)
            spot = place((src0 + row // 16) * 4 + zh * 2 + c, bool(late), xb * 16 + row % 16)
            top = jnp.full((block, LANES), MASKED, F32)
            jobs = []
            for key_late in range(late + 1):
                for g, (ref, low, _) in enumerate(groups):
                    jobs.append((len(jobs), key_late, g, ref, low + TILE * key_late))
            for n, key_late, g, ref, low in jobs:
                keys = tiles(ref, low, TILE)
                found = lax.dot_general(
                    query, keys, (((1,), (1,)), ((), ())), preferred_element_type=F32
                )
                if key_late == late:
                    found = jnp.where(places[key_late][g] <= spot, found, MASKED)
                scores[:, n * 512 : (n + 1) * 512] = found
                for k in range(4):
                    top = jnp.maximum(top, found[:, k * LANES : (k + 1) * LANES])
            top = jnp.max(top, axis=1, keepdims=True)
            total = jnp.zeros((block, LANES), F32)
            summed = jnp.zeros((block, LANES), F32)
            for n, key_late, g, ref, low in jobs:
                weights = jnp.exp2((scores[:, n * 512 : (n + 1) * 512] - top) * log_scale)
                for k in range(4):
                    total = total + weights[:, k * LANES : (k + 1) * LANES]
                values = tiles(ref, low + 64, TILE)
                summed = summed + jnp.dot(
                    weights.astype(BF16), values, preferred_element_type=F32
                )
            result = (summed / jnp.sum(total, axis=1, keepdims=True)).astype(BF16)
            out[src0 : src0 + block // 16, 16 * late : 16 * late + 16, :] = result.reshape(
                block // 16, 16, LANES
            )


def unpack_kernel(came, att, keys, values):
    for n in range(16):
        xa, xb, y = n // 8, (n // 4) % 2, n % 4
        a = xa * 4 + y
        cols = slice(a * LANES, (a + 1) * LANES)
        att[16 * xb : 16 * xb + 16, cols] = came[n, 0:16, :]
        att[TILE + 16 * xb : TILE + 16 * xb + 16, cols] = came[n, 16:32, :]
        for slot in range(2):
            rows = slice((xb * 2 + slot) * TILE, (xb * 2 + slot + 1) * TILE)
            low = 32 + slot * 2 * TILE
            keys[rows, cols] = came[n, low : low + TILE, :]
            values[rows, cols] = came[n, low + TILE : low + 2 * TILE, :]


def shape(dims, dtype=BF16):
    return jax.ShapeDtypeStruct(dims, dtype)


def body(stream, se_pre, se_post, se_taps, mr_pre, mr_post, mr_taps, query, key, value, owner):
    x, y, zh, c = (lax.axis_index(name) for name in CTX)
    me = ((x * 4 + y) * 2 + zh) * 2 + c
    meta = jnp.stack([me, x // 2, x % 2, y, zh, c, c, c]).astype(jnp.int32)
    rows, channels = stream.shape

    odd = c == 1
    early_raw = jnp.concatenate([stream[24:32], se_pre[24:32]], axis=0)
    late_raw = jnp.concatenate([stream[56:64], se_pre[56:64]], axis=0)
    outer = jnp.where(odd, early_raw, late_raw)
    halo_near = lax.ppermute(jnp.where(odd, late_raw, early_raw), "c", SWAP)
    far = ctx_route(jnp.concatenate([key, outer[:, :1024], outer[:, 1024:]], axis=0), across)
    held, halo_near = lax.optimization_barrier((value, halo_near))
    far_values = ctx_route(held, across)
    taps = se_taps.T
    partial = call(
        stats_kernel,
        shape((TILE, LANES), F32),
        [pltpu.VMEM((rows, channels), F32)] * 3 + [pltpu.VMEM((8, channels), F32)],
        [V] * 4,
        flops=15_000_000,
        nbytes=800_000,
        name="stats",
    )(stream, se_pre, se_post, taps)
    sums = call(
        head_kernel,
        shape((TILE, LANES), F32),
        [pltpu.VMEM((2, 16, channels), F32)] + [pltpu.VMEM((2, 8, channels), F32)] * 2 + [pltpu.VMEM((8, channels), F32)],
        [S] + [V] * 7,
        flops=5_000_000,
        nbytes=300_000,
        name="head",
    )(meta, stream, se_pre, se_post, taps, far, halo_near, partial)
    half = sums + lax.ppermute(sums, "tp", [(i, i ^ 1) for i in range(4)])
    packed, half = lax.optimization_barrier((far_values, half))
    other = lax.ppermute(half, "tp", [(i, i ^ 2) for i in range(4)])
    mixed, keep, give = call(
        mix_kernel,
        [shape((rows, channels)), shape((TILE, channels)), shape((TILE, channels))],
        [pltpu.VMEM((2, 40, LANES), F32), pltpu.VMEM((64, LANES), F32), pltpu.VMEM((2, 40, LANES), F32)]
        + [pltpu.VMEM((8, channels), F32)],
        [S] + [V] * 9,
        flops=8_000_000,
        nbytes=3_500_000,
        name="mix",
    )(meta, stream, se_pre, se_post, mr_pre, taps, far, halo_near, half, other)

    got = lax.ppermute(give, "c", SWAP)
    pair = jnp.concatenate([keep, got], axis=0)
    heads = call(
        pack_kernel, shape((16, 288, LANES)), (), [V] * 5, nbytes=2_000_000, name="pack"
    )(key, value, far, packed, query)
    mine = lax.all_to_all(heads, ("x", "y"), 0, 0, tiled=True)
    two = ctx_route(pair, second_chip)
    one = ctx_route(pair, next_chip)
    mark = pair[:16, :128]
    mine, pair = lax.optimization_barrier((mine, pair))
    share = jnp.concatenate([one, two[:TILE]], axis=0)

    rest = lax.ppermute(share, "c", SWAP)
    twin = lax.ppermute(mine, "c", [(0, 1), (1, 0)])

    slots = call(
        slots_kernel, shape((1, 128), jnp.int32), (), [S, V, V], flops=20_000_000_000, nbytes=70_000, name="slots"
    )(meta, owner.reshape(1, 128), owner)
    answered = call(
        attend_kernel,
        shape((16, 160, LANES)),
        [pltpu.VMEM((128, 4096), F32)],
        [S, S, V, V, V],
        flops=1_000_000_000,
        nbytes=3_000_000,
        name="attend",
    )(meta, slots, mine, twin, mark)
    came = lax.all_to_all(answered, ("x", "y"), 0, 0, tiled=True)
    attention_out, cache_keys, cache_values = call(
        unpack_kernel,
        [shape((rows, 1024)), shape((128, 1024)), shape((128, 1024))],
        (),
        [V],
        nbytes=1_300_000,
        name="unpack",
    )(came)
    decode_cache = jnp.stack([cache_keys, cache_values], axis=1)

    reversed_taps = jnp.pad(mr_taps[:, ::-1].astype(F32), ((0, 0), (1, 127)))
    hyena_stream, filter_state = call(
        conv_kernel,
        [shape((rows, channels)), shape((128, channels))],
        [pltpu.VMEM((2, 160, channels), BF16)],
        [S] + [V] * 9,
        flops=100_000_000,
        nbytes=3_000_000,
        name="conv",
    )(meta, reversed_taps, mixed, mr_post, keep, give, got, one, two, rest)
    return hyena_stream, attention_out, decode_cache, filter_state


def solution(mesh):
    fine = Mesh(mesh.devices.reshape(4, 4, 2, 2, 4), (*CTX, "tp"))
    block = P(CTX, "tp")
    in_specs = (block, block, block, P("tp", None), block, block, P("tp", None), block, block, block, P())
    out_specs = (block, block, P(CTX, None, "tp"), block)
    return jax.shard_map(body, mesh=fine, in_specs=in_specs, out_specs=out_specs, check_vma=False)
```

```python
import functools
import math

import jax
import jax.numpy as jnp
from jax import lax
from jax.experimental import pallas as pl
from jax.experimental.pallas import tpu as pltpu
from jax.sharding import Mesh, PartitionSpec as P

HEAD_DIM = 128
CAP = 4
EPS_NORM = 1e-06
MASKED = -1e30
CTX = ("x", "y", "zh", "c")
F32 = jnp.float32
BF16 = jnp.bfloat16
LANES = 128
TILE = 32
TAPS = 7
HALO = 40
PAIRS = tuple((a, b) for a in range(TAPS + 1) for b in range(a, TAPS + 1))


def ctx_route(array, target):
    pairs = [(i, target(i)) for i in range(64) if 0 <= target(i) < 64]
    return lax.ppermute(array, CTX, pairs)


def next_chip(i):
    return 63 if i == 63 else (i + 1 if i % 2 else i - 1)


def across(i):
    return (i + 1 if i % 2 else i - 1) % 64


def second_chip(i):
    return {63: 61, 61: 63}.get(i, i + 3 if i % 2 else i - 3)


SWAP = [(0, 1), (1, 0)]


def call(kernel, out_shape, scratch=(), in_spaces=None, flops=0, nbytes=0, name=None, out_space=pltpu.VMEM, vmem=24):
    specs = [pl.BlockSpec(memory_space=space) for space in in_spaces]
    if isinstance(out_shape, (list, tuple)):
        outs = [pl.BlockSpec(memory_space=pltpu.VMEM) for _ in out_shape]
    else:
        outs = pl.BlockSpec(memory_space=out_space)
    return pl.pallas_call(
        kernel,
        out_shape=out_shape,
        in_specs=specs,
        out_specs=outs,
        scratch_shapes=list(scratch),
        compiler_params=pltpu.CompilerParams(vmem_limit_bytes=vmem * 1024 * 1024),
        cost_estimate=pl.CostEstimate(flops=flops, bytes_accessed=nbytes, transcendentals=0),
        name=name,
    )


V, S = pltpu.VMEM, pltpu.SMEM


def lanes_at(index, width):
    return pl.ds(pl.multiple_of(index * width, width), width)


def halo_rows(meta, far, near, early, step):
    odd = meta[5] == 1
    rows = pl.ds(pl.multiple_of(64 + step // 8 * 16, 16), 16)
    other = far[rows, lanes_at(step % 8, LANES)].astype(F32)
    other = jnp.where(meta[0] == 0, jnp.zeros_like(other), other)
    twin = near[:, lanes_at(step, LANES)].astype(F32)
    before = jnp.where(odd, twin, other)
    after = jnp.where(meta[0] == 63, early, jnp.where(odd, other, twin))
    return before, after


def sum_pairs(out, row, base, tiles, terms_of, packed=None):
    zero = jnp.zeros((8, LANES), F32)
    lane = lax.broadcasted_iota(jnp.int32, (8, LANES), 1)
    packed = zero if packed is None else packed
    for tile in range(tiles):

        def collect(step, sums, tile=tile):
            terms = terms_of(tile, lanes_at(step, LANES))
            return tuple(t + terms[a] * terms[b] for t, (a, b) in zip(sums, PAIRS))

        sums = lax.fori_loop(0, base, collect, (zero,) * len(PAIRS), unroll=4)
        for q, part in enumerate(sums):
            packed = jnp.where(lane == q + 64 * tile, jnp.sum(part, axis=1, keepdims=True), packed)
    out[row : row + 8, :] = packed


def stats_kernel(stream, pre, post, taps, out, us, sf, pf, tf):
    tf[0:TAPS, :] = taps[...].astype(F32)
    chunks = stream.shape[1] // LANES

    def prepare(step, carry):
        cs = lanes_at(step, LANES)
        s = stream[:, cs].astype(F32)
        sf[:, cs] = s
        pf[:, cs] = post[:, cs].astype(F32)
        us[:, cs] = s * pre[:, cs].astype(F32)
        return carry

    lax.fori_loop(0, chunks, prepare, 0, unroll=2)
    out[0:8, :] = jnp.zeros((8, LANES), F32)
    for group in range(1, TILE // 8):

        def terms_of(tile, cs, group=group):
            row = tile * TILE + group * 8
            gate = pf[row : row + 8, cs]
            behind = [us[pl.ds(row - j, 8), cs] for j in range(TAPS)]
            return [sf[row : row + 8, cs]] + [tf[j : j + 1, cs] * gate * behind[j] for j in range(TAPS)]

        sum_pairs(out, group * 8, chunks, 2, terms_of)


def head_kernel(meta, stream, pre, post, taps, far, near, partial, out, us, sf, pf, tf):
    tf[0:TAPS, :] = taps[...].astype(F32)
    chunks = stream.shape[1] // LANES

    def prepare(step, carry):
        cs = lanes_at(step, LANES)
        own = [ref[16:TILE, cs].astype(F32)[8:16] for ref in (stream, pre)]
        halos = halo_rows(meta, far, near, jnp.concatenate(own, axis=0), step)
        squares = []
        for tile in range(2):
            halo = halos[tile]
            rows = slice(tile * TILE, tile * TILE + 16)
            s = stream[rows, cs].astype(F32)[0:8]
            sf[tile, :, cs] = s
            pf[tile, :, cs] = post[rows, cs].astype(F32)[0:8]
            us[tile, 0:8, cs] = halo[0:8] * halo[8:16]
            us[tile, 8:16, cs] = s * pre[rows, cs].astype(F32)[0:8]
            squares.append(carry[tile] + halo[0:8] * halo[0:8])
        return tuple(squares)

    zero = jnp.zeros((8, LANES), F32)
    squares = lax.fori_loop(0, chunks, prepare, (zero, zero), unroll=2)
    lane = lax.broadcasted_iota(jnp.int32, (8, LANES), 1)
    packed = zero
    for tile in range(2):
        packed = jnp.where(lane == HALO + 64 * tile, jnp.sum(squares[tile], axis=1, keepdims=True), packed)

    def terms_of(tile, cs):
        gate = pf[tile, :, cs]
        behind = [us[tile, pl.ds(8 - j, 8), cs] for j in range(TAPS)]
        return [sf[tile, :, cs]] + [tf[j : j + 1, cs] * gate * behind[j] for j in range(TAPS)]

    sum_pairs(out, 0, chunks, 2, terms_of, packed)
    out[8:TILE, :] = partial[8:TILE, :]


def pack_kernel(k, v, far, far_values, q, out):
    for a in range(8):
        cols = slice(a * LANES, (a + 1) * LANES)
        for xb in range(2):
            n = ((a // 4) * 2 + xb) * 4 + a % 4
            out[n, 0:64, :] = k[:, cols]
            out[n, 64:128, :] = v[:, cols]
            out[n, 128:192, :] = far[0:64, cols]
            out[n, 192:256, :] = far_values[:, cols]
            for t in range(2):
                low = TILE * t + 16 * xb
                out[n, 256 + 16 * t : 272 + 16 * t, :] = q[low : low + 16, cols]


def mix_kernel(
    meta, stream, pre, post, mrpre, taps, he, hl, half, other, mixed, keep, give,
    sc, s2, xs, tf,
):
    odd = meta[5] == 1
    tf[0:TAPS, :] = taps[...].astype(F32)
    width = 1.0 / 8192.0
    total = half[...] + other[...]
    scale = lax.rsqrt(total * width + EPS_NORM)
    for tile in range(2):
        near = 64 * tile
        far = near + HALO
        sc[tile, 0:8, :] = jnp.broadcast_to(scale[0:8, far : far + 1], (8, LANES))
        sc[tile, 8:40, :] = jnp.broadcast_to(scale[:, near : near + 1], (TILE, LANES))
    lane = lax.broadcasted_iota(jnp.int32, (TILE, LANES), 1)
    for tile in range(2):
        factor = [jnp.ones((TILE, LANES), F32)]
        for j in range(TAPS):
            factor.append(sc[tile, pl.ds(8 - j, TILE), :])
        weight = jnp.zeros((TILE, LANES), F32)
        for q, (a, b) in enumerate(PAIRS):
            term = factor[a] * factor[b]
            weight = jnp.where(lane == q + 64 * tile, term if a == b else term * 2.0, weight)
        rows = slice(tile * TILE, (tile + 1) * TILE)
        squares = jnp.sum(weight * total, axis=1, keepdims=True)
        second = lax.rsqrt(jnp.maximum(squares, 0.0) * width + EPS_NORM)
        s2[rows, :] = jnp.broadcast_to(second, (TILE, LANES))

    def one(step, carry):
        cs = lanes_at(step, LANES)
        s = stream[:, cs].astype(F32)
        p = pre[:, cs].astype(F32)
        u = s * p
        own = jnp.concatenate([s[TILE - 8 : TILE], p[TILE - 8 : TILE]], axis=0)
        before, after = halo_rows(meta, he, hl, own, step)
        eu, lu = before[0:8] * before[8:16], after[0:8] * after[8:16]
        gate = post[:, cs].astype(F32)
        front = mrpre[:, cs].astype(F32)
        for tile, halo in enumerate((eu, lu)):
            rows = slice(tile * TILE, (tile + 1) * TILE)
            xs[tile, 0:8, :] = (halo * sc[tile, 0:8, :]).astype(BF16).astype(F32)
            xs[tile, 8:40, :] = (u[rows] * sc[tile, 8:40, :]).astype(BF16).astype(F32)
        values = []
        for tile in range(2):
            rows = slice(tile * TILE, (tile + 1) * TILE)
            acc = jnp.zeros((TILE, LANES), F32)
            for j in range(TAPS):
                acc = acc + tf[j : j + 1, cs] * xs[tile, pl.ds(8 - j, TILE), :]
            value = (s[rows] + gate[rows] * acc).astype(BF16)
            mixed[rows, cs] = value
            values.append((front[rows] * value.astype(F32) * s2[rows, :]).astype(BF16))
        keep[:, cs] = jnp.where(odd, values[0], values[1])
        give[:, cs] = jnp.where(odd, values[1], values[0])
        return carry

    lax.fori_loop(0, stream.shape[1] // LANES, one, 0)


def conv_kernel(meta, taps, mixed, post, keep, give, got, one, two, rest, out, state, ext):
    ext[0, 0:32, :] = two[32:64, :]
    ext[0, 32:64, :] = two[0:32, :]
    ext[0, 64:96, :] = one[32:64, :]
    ext[0, 96:128, :] = one[0:32, :]
    ext[0, 128:160, :] = give[...]
    ext[1, 0:32, :] = rest[64:96, :]
    ext[1, 32:64, :] = rest[32:64, :]
    ext[1, 64:96, :] = rest[0:32, :]
    ext[1, 96:128, :] = got[...]
    ext[1, 128:160, :] = keep[...]
    group_width = out.shape[1] // taps.shape[0]
    for g in range(taps.shape[0]):
        row = jnp.broadcast_to(taps[g : g + 1, :], (TILE, 256))
        toeplitz = pltpu.roll(row, 0, 1, stride=1, stride_axis=0)[:, 0:160].astype(BF16)
        cols = slice(g * group_width, (g + 1) * group_width)
        for part in range(2):
            place = meta[5] if part == 0 else 1 - meta[5]
            rows = pl.ds(pl.multiple_of(place * TILE, TILE), TILE)
            acc = jnp.dot(toeplitz, ext[part, :, cols], preferred_element_type=F32)
            value = mixed[rows, cols].astype(F32) + post[rows, cols].astype(F32) * acc
            out[rows, cols] = value.astype(BF16)

    @pl.when(meta[0] == 0)
    def _():
        state[...] = ext[1, 32:160, :]

    @pl.when(meta[0] != 0)
    def _():
        state[...] = jnp.zeros_like(state)


def slots_kernel(meta, owner_row, owner_col, out):
    xb, zh, c = meta[2], meta[4], meta[5]
    row = lax.broadcasted_iota(jnp.int32, (128, 128), 0)
    col = lax.broadcasted_iota(jnp.int32, (128, 128), 1)
    mine = owner_col[...]
    before = (owner_row[...] == mine) & (col < row)
    rank = jnp.sum(jnp.where(before, 1, 0), axis=1, keepdims=True)
    want = (col // 2 * 4 + zh * 2 + c) * CAP + xb * 2 + col % 2
    found = (mine * CAP + rank == want) & (col < 32)
    tile = jnp.sum(jnp.where(found, row + 1, 0), axis=0, keepdims=True) - 1
    held = jnp.maximum(tile, 0)
    late = held >= 64
    device = jnp.where(late, 127 - held, held)
    across_z = (device >> 1 & 1) != zh
    holder = jnp.where(across_z, (device + jnp.where(device & 1 == 1, 1, 63)) & 63, device)
    out[0:1, :] = holder >> 2
    out[1:2, :] = jnp.where(across_z, 128, 0) + jnp.where(late, TILE, 0)
    out[2:3, :] = jnp.where((holder & 1) == c, 1, 0)
    out[3:4, :] = jnp.where(tile >= 0, 1, 0)


def attend_kernel(meta, slots, mine, twin, after, out, scores):
    xb, zh, c = meta[2], meta[4], meta[5]

    def pieces(n, carry):
        for slot in range(2):
            at = n * 2 + slot
            src, low = slots[0, at], slots[1, at]
            near, there = slots[2, at] == 1, slots[3, at] == 1
            for kv in range(2):
                rows = pl.ds(pl.multiple_of(low + 64 * kv, TILE), TILE)
                value = jnp.where(near, mine[src, rows, :], twin[src, rows, :])
                value = jnp.where(there, value, jnp.zeros_like(value))
                first = 32 + (slot * 2 + kv) * TILE
                out[n, first : first + TILE, :] = value
        return carry

    lax.fori_loop(0, 16, pieces, 0, unroll=16)
    log_scale = math.log2(math.e) / math.sqrt(HEAD_DIM)
    def owner(core, far):
        def of(src):
            device = src * 4 + zh * 2 + core
            return (jnp.where(core == 1, device + 1, device + 63) % 64) if far else device

        return of

    groups = [(ref, 128 * far, owner(core, far)) for ref, core in ((mine, c), (twin, 1 - c)) for far in range(2)]

    def place(device, late, u):
        return (127 - device if late else device) * TILE + u

    def columns(late):
        col = lax.broadcasted_iota(jnp.int32, (1, 512), 1)
        return [place(of(col // TILE), late, col % TILE) for _, _, of in groups]

    def tiles(ref, low, count):
        return ref[:, low : low + count, :].reshape(16 * count, LANES)

    block = 128
    places = (columns(False), columns(True))
    for late in range(2):
        for part in range(256 // block):
            src0 = part * (block // 16)
            query = mine[src0 : src0 + block // 16, 256 + 16 * late : 272 + 16 * late, :]
            query = query.reshape(block, LANES)
            row = lax.broadcasted_iota(jnp.int32, (block, 1), 0)
            spot = place((src0 + row // 16) * 4 + zh * 2 + c, bool(late), xb * 16 + row % 16)
            top = jnp.full((block, LANES), MASKED, F32)
            jobs = []
            for key_late in range(late + 1):
                for g, (ref, low, _) in enumerate(groups):
                    jobs.append((len(jobs), key_late, g, ref, low + TILE * key_late))
            for n, key_late, g, ref, low in jobs:
                keys = tiles(ref, low, TILE)
                found = lax.dot_general(
                    query, keys, (((1,), (1,)), ((), ())), preferred_element_type=F32
                )
                if key_late == late:
                    found = jnp.where(places[key_late][g] <= spot, found, MASKED)
                scores[:, n * 512 : (n + 1) * 512] = found
                for k in range(4):
                    top = jnp.maximum(top, found[:, k * LANES : (k + 1) * LANES])
            top = jnp.max(top, axis=1, keepdims=True)
            total = jnp.zeros((block, LANES), F32)
            summed = jnp.zeros((block, LANES), F32)
            for n, key_late, g, ref, low in jobs:
                weights = jnp.exp2((scores[:, n * 512 : (n + 1) * 512] - top) * log_scale)
                for k in range(4):
                    total = total + weights[:, k * LANES : (k + 1) * LANES]
                values = tiles(ref, low + 64, TILE)
                summed = summed + jnp.dot(
                    weights.astype(BF16), values, preferred_element_type=F32
                )
            result = (summed / jnp.sum(total, axis=1, keepdims=True)).astype(BF16)
            out[src0 : src0 + block // 16, 16 * late : 16 * late + 16, :] = result.reshape(
                block // 16, 16, LANES
            )


def unpack_kernel(came, att, keys, values):
    for n in range(16):
        xa, xb, y = n // 8, (n // 4) % 2, n % 4
        a = xa * 4 + y
        cols = slice(a * LANES, (a + 1) * LANES)
        att[16 * xb : 16 * xb + 16, cols] = came[n, 0:16, :]
        att[TILE + 16 * xb : TILE + 16 * xb + 16, cols] = came[n, 16:32, :]
        for slot in range(2):
            rows = slice((xb * 2 + slot) * TILE, (xb * 2 + slot + 1) * TILE)
            low = 32 + slot * 2 * TILE
            keys[rows, cols] = came[n, low : low + TILE, :]
            values[rows, cols] = came[n, low + TILE : low + 2 * TILE, :]


def shape(dims, dtype=BF16):
    return jax.ShapeDtypeStruct(dims, dtype)


def body(stream, se_pre, se_post, se_taps, mr_pre, mr_post, mr_taps, query, key, value, owner):
    x, y, zh, c = (lax.axis_index(name) for name in CTX)
    me = ((x * 4 + y) * 2 + zh) * 2 + c
    meta = jnp.stack([me, x // 2, x % 2, y, zh, c, c, c]).astype(jnp.int32)
    rows, channels = stream.shape

    odd = c == 1
    early_raw = jnp.concatenate([stream[24:32], se_pre[24:32]], axis=0)
    late_raw = jnp.concatenate([stream[56:64], se_pre[56:64]], axis=0)
    outer = jnp.where(odd, early_raw, late_raw)
    halo_near = lax.ppermute(jnp.where(odd, late_raw, early_raw), "c", SWAP)
    far = ctx_route(jnp.concatenate([key, outer[:, :1024], outer[:, 1024:]], axis=0), across)
    held, halo_near = lax.optimization_barrier((value, halo_near))
    far_values = ctx_route(held, across)
    taps = se_taps.T
    partial = call(
        stats_kernel,
        shape((TILE, LANES), F32),
        [pltpu.VMEM((rows, channels), F32)] * 3 + [pltpu.VMEM((8, channels), F32)],
        [V] * 4,
        flops=15_000_000,
        nbytes=800_000,
        name="stats",
    )(stream, se_pre, se_post, taps)
    sums = call(
        head_kernel,
        shape((TILE, LANES), F32),
        [pltpu.VMEM((2, 16, channels), F32)] + [pltpu.VMEM((2, 8, channels), F32)] * 2 + [pltpu.VMEM((8, channels), F32)],
        [S] + [V] * 7,
        flops=5_000_000,
        nbytes=300_000,
        name="head",
    )(meta, stream, se_pre, se_post, taps, far, halo_near, partial)
    half = sums + lax.ppermute(sums, "tp", [(i, i ^ 1) for i in range(4)])
    packed, half = lax.optimization_barrier((far_values, half))
    other = lax.ppermute(half, "tp", [(i, i ^ 2) for i in range(4)])
    mixed, keep, give = call(
        mix_kernel,
        [shape((rows, channels)), shape((TILE, channels)), shape((TILE, channels))],
        [pltpu.VMEM((2, 40, LANES), F32), pltpu.VMEM((64, LANES), F32), pltpu.VMEM((2, 40, LANES), F32)]
        + [pltpu.VMEM((8, channels), F32)],
        [S] + [V] * 9,
        flops=20_000_000_000,
        nbytes=3_500_000,
        name="mix",
    )(meta, stream, se_pre, se_post, mr_pre, taps, far, halo_near, half, other)

    got = lax.ppermute(give, "c", SWAP)
    pair = jnp.concatenate([keep, got], axis=0)
    heads = call(
        pack_kernel, shape((16, 288, LANES)), (), [V] * 5, nbytes=2_000_000, name="pack"
    )(key, value, far, packed, query)
    mine = lax.all_to_all(heads, ("x", "y"), 0, 0, tiled=True)
    two = ctx_route(pair, second_chip)
    one = ctx_route(pair, next_chip)
    mark = pair[:16, :128]
    mine, pair = lax.optimization_barrier((mine, pair))
    share = jnp.concatenate([one, two[:TILE]], axis=0)

    rest = lax.ppermute(share, "c", SWAP)
    twin = lax.ppermute(mine, "c", [(0, 1), (1, 0)])

    slots = call(
        slots_kernel, shape((4, 128), jnp.int32), (), [S, V, V], flops=20_000_000_000, nbytes=70_000, name="slots"
    )(meta, owner.reshape(1, 128), owner)
    answered = call(
        attend_kernel,
        shape((16, 160, LANES)),
        [pltpu.VMEM((128, 4096), F32)],
        [S, S, V, V, V],
        flops=1_000_000_000,
        nbytes=3_000_000,
        name="attend",
    )(meta, slots, mine, twin, mark)
    came = lax.all_to_all(answered, ("x", "y"), 0, 0, tiled=True)
    attention_out, cache_keys, cache_values = call(
        unpack_kernel,
        [shape((rows, 1024)), shape((128, 1024)), shape((128, 1024))],
        (),
        [V],
        nbytes=1_300_000,
        name="unpack",
    )(came)
    decode_cache = jnp.stack([cache_keys, cache_values], axis=1)

    reversed_taps = jnp.pad(mr_taps[:, ::-1].astype(F32), ((0, 0), (1, 127)))
    hyena_stream, filter_state = call(
        conv_kernel,
        [shape((rows, channels)), shape((128, channels))],
        [pltpu.VMEM((2, 160, channels), BF16)],
        [S] + [V] * 9,
        flops=100_000_000,
        nbytes=3_000_000,
        name="conv",
    )(meta, reversed_taps, mixed, mr_post, keep, give, got, one, two, rest)
    return hyena_stream, attention_out, decode_cache, filter_state


def solution(mesh):
    fine = Mesh(mesh.devices.reshape(4, 4, 2, 2, 4), (*CTX, "tp"))
    block = P(CTX, "tp")
    in_specs = (block, block, block, P("tp", None), block, block, P("tp", None), block, block, block, P())
    out_specs = (block, block, P(CTX, None, "tp"), block)
    return jax.shard_map(body, mesh=fine, in_specs=in_specs, out_specs=out_specs, check_vma=False)
```

```python
import functools
import math

import jax
import jax.numpy as jnp
from jax import lax
from jax.experimental import pallas as pl
from jax.experimental.pallas import tpu as pltpu
from jax.sharding import Mesh, PartitionSpec as P

HEAD_DIM = 128
CAP = 4
EPS_NORM = 1e-06
MASKED = -1e30
CTX = ("x", "y", "zh", "c")
F32 = jnp.float32
BF16 = jnp.bfloat16
LANES = 128
TILE = 32
TAPS = 7
HALO = 40
PAIRS = tuple((a, b) for a in range(TAPS + 1) for b in range(a, TAPS + 1))


def ctx_route(array, target):
    pairs = [(i, target(i)) for i in range(64) if 0 <= target(i) < 64]
    return lax.ppermute(array, CTX, pairs)


def next_chip(i):
    return 63 if i == 63 else (i + 1 if i % 2 else i - 1)


def across(i):
    return (i + 1 if i % 2 else i - 1) % 64


def second_chip(i):
    return {63: 61, 61: 63}.get(i, i + 3 if i % 2 else i - 3)


SWAP = [(0, 1), (1, 0)]


def call(kernel, out_shape, scratch=(), in_spaces=None, flops=0, nbytes=0, name=None, out_space=pltpu.VMEM, vmem=24):
    specs = [pl.BlockSpec(memory_space=space) for space in in_spaces]
    if isinstance(out_shape, (list, tuple)):
        outs = [pl.BlockSpec(memory_space=pltpu.VMEM) for _ in out_shape]
    else:
        outs = pl.BlockSpec(memory_space=out_space)
    return pl.pallas_call(
        kernel,
        out_shape=out_shape,
        in_specs=specs,
        out_specs=outs,
        scratch_shapes=list(scratch),
        compiler_params=pltpu.CompilerParams(vmem_limit_bytes=vmem * 1024 * 1024),
        cost_estimate=pl.CostEstimate(flops=flops, bytes_accessed=nbytes, transcendentals=0),
        name=name,
    )


V, S = pltpu.VMEM, pltpu.SMEM


def lanes_at(index, width):
    return pl.ds(pl.multiple_of(index * width, width), width)


def halo_rows(meta, far, near, early, step):
    odd = meta[5] == 1
    rows = pl.ds(pl.multiple_of(64 + step // 8 * 16, 16), 16)
    other = far[rows, lanes_at(step % 8, LANES)].astype(F32)
    other = jnp.where(meta[0] == 0, jnp.zeros_like(other), other)
    twin = near[:, lanes_at(step, LANES)].astype(F32)
    before = jnp.where(odd, twin, other)
    after = jnp.where(meta[0] == 63, early, jnp.where(odd, other, twin))
    return before, after


def sum_pairs(out, row, base, tiles, terms_of, packed=None):
    zero = jnp.zeros((8, LANES), F32)
    lane = lax.broadcasted_iota(jnp.int32, (8, LANES), 1)
    packed = zero if packed is None else packed
    for tile in range(tiles):

        def collect(step, sums, tile=tile):
            terms = terms_of(tile, lanes_at(step, LANES))
            return tuple(t + terms[a] * terms[b] for t, (a, b) in zip(sums, PAIRS))

        sums = lax.fori_loop(0, base, collect, (zero,) * len(PAIRS), unroll=4)
        for q, part in enumerate(sums):
            packed = jnp.where(lane == q + 64 * tile, jnp.sum(part, axis=1, keepdims=True), packed)
    out[row : row + 8, :] = packed


def stats_kernel(stream, pre, post, taps, out, us, sf, pf, tf):
    tf[0:TAPS, :] = taps[...].astype(F32)
    chunks = stream.shape[1] // LANES

    def prepare(step, carry):
        cs = lanes_at(step, LANES)
        s = stream[:, cs].astype(F32)
        sf[:, cs] = s
        pf[:, cs] = post[:, cs].astype(F32)
        us[:, cs] = s * pre[:, cs].astype(F32)
        return carry

    lax.fori_loop(0, chunks, prepare, 0, unroll=2)
    out[0:8, :] = jnp.zeros((8, LANES), F32)
    for group in range(1, TILE // 8):

        def terms_of(tile, cs, group=group):
            row = tile * TILE + group * 8
            gate = pf[row : row + 8, cs]
            behind = [us[pl.ds(row - j, 8), cs] for j in range(TAPS)]
            return [sf[row : row + 8, cs]] + [tf[j : j + 1, cs] * gate * behind[j] for j in range(TAPS)]

        sum_pairs(out, group * 8, chunks, 2, terms_of)


def head_kernel(meta, stream, pre, post, taps, far, near, partial, out, us, sf, pf, tf):
    tf[0:TAPS, :] = taps[...].astype(F32)
    chunks = stream.shape[1] // LANES

    def prepare(step, carry):
        cs = lanes_at(step, LANES)
        own = [ref[16:TILE, cs].astype(F32)[8:16] for ref in (stream, pre)]
        halos = halo_rows(meta, far, near, jnp.concatenate(own, axis=0), step)
        squares = []
        for tile in range(2):
            halo = halos[tile]
            rows = slice(tile * TILE, tile * TILE + 16)
            s = stream[rows, cs].astype(F32)[0:8]
            sf[tile, :, cs] = s
            pf[tile, :, cs] = post[rows, cs].astype(F32)[0:8]
            us[tile, 0:8, cs] = halo[0:8] * halo[8:16]
            us[tile, 8:16, cs] = s * pre[rows, cs].astype(F32)[0:8]
            squares.append(carry[tile] + halo[0:8] * halo[0:8])
        return tuple(squares)

    zero = jnp.zeros((8, LANES), F32)
    squares = lax.fori_loop(0, chunks, prepare, (zero, zero), unroll=2)
    lane = lax.broadcasted_iota(jnp.int32, (8, LANES), 1)
    packed = zero
    for tile in range(2):
        packed = jnp.where(lane == HALO + 64 * tile, jnp.sum(squares[tile], axis=1, keepdims=True), packed)

    def terms_of(tile, cs):
        gate = pf[tile, :, cs]
        behind = [us[tile, pl.ds(8 - j, 8), cs] for j in range(TAPS)]
        return [sf[tile, :, cs]] + [tf[j : j + 1, cs] * gate * behind[j] for j in range(TAPS)]

    sum_pairs(out, 0, chunks, 2, terms_of, packed)
    out[8:TILE, :] = partial[8:TILE, :]


def pack_kernel(k, v, far, far_values, q, out):
    for a in range(8):
        cols = slice(a * LANES, (a + 1) * LANES)
        for xb in range(2):
            n = ((a // 4) * 2 + xb) * 4 + a % 4
            out[n, 0:64, :] = k[:, cols]
            out[n, 64:128, :] = v[:, cols]
            out[n, 128:192, :] = far[0:64, cols]
            out[n, 192:256, :] = far_values[:, cols]
            for t in range(2):
                low = TILE * t + 16 * xb
                out[n, 256 + 16 * t : 272 + 16 * t, :] = q[low : low + 16, cols]


def mix_kernel(
    meta, stream, pre, post, mrpre, taps, he, hl, half, other, mixed, keep, give,
    sc, s2, xs, tf,
):
    odd = meta[5] == 1
    tf[0:TAPS, :] = taps[...].astype(F32)
    width = 1.0 / 8192.0
    total = half[...] + other[...]
    scale = lax.rsqrt(total * width + EPS_NORM)
    for tile in range(2):
        near = 64 * tile
        far = near + HALO
        sc[tile, 0:8, :] = jnp.broadcast_to(scale[0:8, far : far + 1], (8, LANES))
        sc[tile, 8:40, :] = jnp.broadcast_to(scale[:, near : near + 1], (TILE, LANES))
    lane = lax.broadcasted_iota(jnp.int32, (TILE, LANES), 1)
    for tile in range(2):
        factor = [jnp.ones((TILE, LANES), F32)]
        for j in range(TAPS):
            factor.append(sc[tile, pl.ds(8 - j, TILE), :])
        weight = jnp.zeros((TILE, LANES), F32)
        for q, (a, b) in enumerate(PAIRS):
            term = factor[a] * factor[b]
            weight = jnp.where(lane == q + 64 * tile, term if a == b else term * 2.0, weight)
        rows = slice(tile * TILE, (tile + 1) * TILE)
        squares = jnp.sum(weight * total, axis=1, keepdims=True)
        second = lax.rsqrt(jnp.maximum(squares, 0.0) * width + EPS_NORM)
        s2[rows, :] = jnp.broadcast_to(second, (TILE, LANES))

    def one(step, carry):
        cs = lanes_at(step, LANES)
        s = stream[:, cs].astype(F32)
        p = pre[:, cs].astype(F32)
        u = s * p
        own = jnp.concatenate([s[TILE - 8 : TILE], p[TILE - 8 : TILE]], axis=0)
        before, after = halo_rows(meta, he, hl, own, step)
        eu, lu = before[0:8] * before[8:16], after[0:8] * after[8:16]
        gate = post[:, cs].astype(F32)
        front = mrpre[:, cs].astype(F32)
        for tile, halo in enumerate((eu, lu)):
            rows = slice(tile * TILE, (tile + 1) * TILE)
            xs[tile, 0:8, :] = (halo * sc[tile, 0:8, :]).astype(BF16).astype(F32)
            xs[tile, 8:40, :] = (u[rows] * sc[tile, 8:40, :]).astype(BF16).astype(F32)
        values = []
        for tile in range(2):
            rows = slice(tile * TILE, (tile + 1) * TILE)
            acc = jnp.zeros((TILE, LANES), F32)
            for j in range(TAPS):
                acc = acc + tf[j : j + 1, cs] * xs[tile, pl.ds(8 - j, TILE), :]
            value = (s[rows] + gate[rows] * acc).astype(BF16)
            mixed[rows, cs] = value
            values.append((front[rows] * value.astype(F32) * s2[rows, :]).astype(BF16))
        keep[:, cs] = jnp.where(odd, values[0], values[1])
        give[:, cs] = jnp.where(odd, values[1], values[0])
        return carry

    lax.fori_loop(0, stream.shape[1] // LANES, one, 0)


def conv_kernel(meta, taps, mixed, post, keep, give, got, one, two, rest, out, state, ext):
    ext[0, 0:32, :] = two[32:64, :]
    ext[0, 32:64, :] = two[0:32, :]
    ext[0, 64:96, :] = one[32:64, :]
    ext[0, 96:128, :] = one[0:32, :]
    ext[0, 128:160, :] = give[...]
    ext[1, 0:32, :] = rest[64:96, :]
    ext[1, 32:64, :] = rest[32:64, :]
    ext[1, 64:96, :] = rest[0:32, :]
    ext[1, 96:128, :] = got[...]
    ext[1, 128:160, :] = keep[...]
    group_width = out.shape[1] // taps.shape[0]
    for g in range(taps.shape[0]):
        row = jnp.broadcast_to(taps[g : g + 1, :], (TILE, 256))
        toeplitz = pltpu.roll(row, 0, 1, stride=1, stride_axis=0)[:, 0:160].astype(BF16)
        cols = slice(g * group_width, (g + 1) * group_width)
        for part in range(2):
            place = meta[5] if part == 0 else 1 - meta[5]
            rows = pl.ds(pl.multiple_of(place * TILE, TILE), TILE)
            acc = jnp.dot(toeplitz, ext[part, :, cols], preferred_element_type=F32)
            value = mixed[rows, cols].astype(F32) + post[rows, cols].astype(F32) * acc
            out[rows, cols] = value.astype(BF16)

    @pl.when(meta[0] == 0)
    def _():
        state[...] = ext[1, 32:160, :]

    @pl.when(meta[0] != 0)
    def _():
        state[...] = jnp.zeros_like(state)


def slots_kernel(meta, owner_row, owner_col, out):
    xb, zh, c = meta[2], meta[4], meta[5]
    row = lax.broadcasted_iota(jnp.int32, (128, 128), 0)
    col = lax.broadcasted_iota(jnp.int32, (128, 128), 1)
    mine = owner_col[...]
    before = (owner_row[...] == mine) & (col < row)
    rank = jnp.sum(jnp.where(before, 1, 0), axis=1, keepdims=True)
    want = (col // 2 * 4 + zh * 2 + c) * CAP + xb * 2 + col % 2
    found = (mine * CAP + rank == want) & (col < 32)
    tile = jnp.sum(jnp.where(found, row + 1, 0), axis=0, keepdims=True) - 1
    held = jnp.maximum(tile, 0)
    late = held >= 64
    device = jnp.where(late, 127 - held, held)
    across_z = (device >> 1 & 1) != zh
    holder = jnp.where(across_z, (device + jnp.where(device & 1 == 1, 1, 63)) & 63, device)
    out[0:1, :] = holder >> 2
    out[1:2, :] = jnp.where(across_z, 128, 0) + jnp.where(late, TILE, 0)
    out[2:3, :] = jnp.where((holder & 1) == c, 1, 0)
    out[3:4, :] = jnp.where(tile >= 0, 1, 0)


def attend_kernel(meta, slots, mine, twin, after, out, scores):
    xb, zh, c = meta[2], meta[4], meta[5]

    def pieces(n, carry):
        for slot in range(2):
            at = n * 2 + slot
            src, low = slots[0, at], slots[1, at]
            near, there = slots[2, at] == 1, slots[3, at] == 1
            for kv in range(2):
                rows = pl.ds(pl.multiple_of(low + 64 * kv, TILE), TILE)
                value = jnp.where(near, mine[src, rows, :], twin[src, rows, :])
                value = jnp.where(there, value, jnp.zeros_like(value))
                first = 32 + (slot * 2 + kv) * TILE
                out[n, first : first + TILE, :] = value
        return carry

    lax.fori_loop(0, 16, pieces, 0, unroll=16)
    log_scale = math.log2(math.e) / math.sqrt(HEAD_DIM)
    def owner(core, far):
        def of(src):
            device = src * 4 + zh * 2 + core
            return (jnp.where(core == 1, device + 1, device + 63) % 64) if far else device

        return of

    groups = [(ref, 128 * far, owner(core, far)) for ref, core in ((mine, c), (twin, 1 - c)) for far in range(2)]

    def place(device, late, u):
        return (127 - device if late else device) * TILE + u

    def columns(late):
        col = lax.broadcasted_iota(jnp.int32, (1, 512), 1)
        return [place(of(col // TILE), late, col % TILE) for _, _, of in groups]

    def tiles(ref, low, count):
        return ref[:, low : low + count, :].reshape(16 * count, LANES)

    block = 256
    places = (columns(False), columns(True))
    for late in range(2):
        for part in range(256 // block):
            src0 = part * (block // 16)
            query = mine[src0 : src0 + block // 16, 256 + 16 * late : 272 + 16 * late, :]
            query = query.reshape(block, LANES)
            row = lax.broadcasted_iota(jnp.int32, (block, 1), 0)
            spot = place((src0 + row // 16) * 4 + zh * 2 + c, bool(late), xb * 16 + row % 16)
            top = jnp.full((block, LANES), MASKED, F32)
            jobs = []
            for key_late in range(late + 1):
                for g, (ref, low, _) in enumerate(groups):
                    jobs.append((len(jobs), key_late, g, ref, low + TILE * key_late))
            for n, key_late, g, ref, low in jobs:
                keys = tiles(ref, low, TILE)
                found = lax.dot_general(
                    query, keys, (((1,), (1,)), ((), ())), preferred_element_type=F32
                )
                if key_late == late:
                    found = jnp.where(places[key_late][g] <= spot, found, MASKED)
                scores[:, n * 512 : (n + 1) * 512] = found
                for k in range(4):
                    top = jnp.maximum(top, found[:, k * LANES : (k + 1) * LANES])
            top = jnp.max(top, axis=1, keepdims=True)
            total = jnp.zeros((block, LANES), F32)
            summed = jnp.zeros((block, LANES), F32)
            for n, key_late, g, ref, low in jobs:
                weights = jnp.exp2((scores[:, n * 512 : (n + 1) * 512] - top) * log_scale)
                for k in range(4):
                    total = total + weights[:, k * LANES : (k + 1) * LANES]
                values = tiles(ref, low + 64, TILE)
                summed = summed + jnp.dot(
                    weights.astype(BF16), values, preferred_element_type=F32
                )
            result = (summed / jnp.sum(total, axis=1, keepdims=True)).astype(BF16)
            out[src0 : src0 + block // 16, 16 * late : 16 * late + 16, :] = result.reshape(
                block // 16, 16, LANES
            )


def unpack_kernel(came, att, cache):
    for n in range(16):
        xa, xb, y = n // 8, (n // 4) % 2, n % 4
        a = xa * 4 + y
        cols = slice(a * LANES, (a + 1) * LANES)
        att[16 * xb : 16 * xb + 16, cols] = came[n, 0:16, :]
        att[TILE + 16 * xb : TILE + 16 * xb + 16, cols] = came[n, 16:32, :]
        for slot in range(2):
            rows = slice((xb * 2 + slot) * TILE, (xb * 2 + slot + 1) * TILE)
            low = 32 + slot * 2 * TILE
            cache[rows, 0, cols] = came[n, low : low + TILE, :]
            cache[rows, 1, cols] = came[n, low + TILE : low + 2 * TILE, :]


def shape(dims, dtype=BF16):
    return jax.ShapeDtypeStruct(dims, dtype)


def body(stream, se_pre, se_post, se_taps, mr_pre, mr_post, mr_taps, query, key, value, owner):
    x, y, zh, c = (lax.axis_index(name) for name in CTX)
    me = ((x * 4 + y) * 2 + zh) * 2 + c
    meta = jnp.stack([me, x // 2, x % 2, y, zh, c, c, c]).astype(jnp.int32)
    rows, channels = stream.shape

    odd = c == 1
    early_raw = jnp.concatenate([stream[24:32], se_pre[24:32]], axis=0)
    late_raw = jnp.concatenate([stream[56:64], se_pre[56:64]], axis=0)
    outer = jnp.where(odd, early_raw, late_raw)
    halo_near = lax.ppermute(jnp.where(odd, late_raw, early_raw), "c", SWAP)
    far = ctx_route(jnp.concatenate([key, outer[:, :1024], outer[:, 1024:]], axis=0), across)
    held, halo_near = lax.optimization_barrier((value, halo_near))
    far_values = ctx_route(held, across)
    taps = se_taps.T
    partial = call(
        stats_kernel,
        shape((TILE, LANES), F32),
        [pltpu.VMEM((rows, channels), F32)] * 3 + [pltpu.VMEM((8, channels), F32)],
        [V] * 4,
        flops=15_000_000,
        nbytes=800_000,
        name="stats",
    )(stream, se_pre, se_post, taps)
    sums = call(
        head_kernel,
        shape((TILE, LANES), F32),
        [pltpu.VMEM((2, 16, channels), F32)] + [pltpu.VMEM((2, 8, channels), F32)] * 2 + [pltpu.VMEM((8, channels), F32)],
        [S] + [V] * 7,
        flops=5_000_000,
        nbytes=300_000,
        name="head",
    )(meta, stream, se_pre, se_post, taps, far, halo_near, partial)
    half = sums + lax.ppermute(sums, "tp", [(i, i ^ 1) for i in range(4)])
    packed, half = lax.optimization_barrier((far_values, half))
    other = lax.ppermute(half, "tp", [(i, i ^ 2) for i in range(4)])
    mixed, keep, give = call(
        mix_kernel,
        [shape((rows, channels)), shape((TILE, channels)), shape((TILE, channels))],
        [pltpu.VMEM((2, 40, LANES), F32), pltpu.VMEM((64, LANES), F32), pltpu.VMEM((2, 40, LANES), F32)]
        + [pltpu.VMEM((8, channels), F32)],
        [S] + [V] * 9,
        flops=20_000_000_000,
        nbytes=3_500_000,
        name="mix",
    )(meta, stream, se_pre, se_post, mr_pre, taps, far, halo_near, half, other)

    got = lax.ppermute(give, "c", SWAP)
    pair = jnp.concatenate([keep, got], axis=0)
    heads = call(
        pack_kernel, shape((16, 288, LANES)), (), [V] * 5, nbytes=2_000_000, name="pack"
    )(key, value, far, packed, query)
    mine = lax.all_to_all(heads, ("x", "y"), 0, 0, tiled=True)
    two = ctx_route(pair, second_chip)
    one = ctx_route(pair, next_chip)
    mark = pair[:16, :128]
    mine, pair = lax.optimization_barrier((mine, pair))
    share = jnp.concatenate([one, two[:TILE]], axis=0)

    rest = lax.ppermute(share, "c", SWAP)
    twin = lax.ppermute(mine, "c", [(0, 1), (1, 0)])

    slots = call(
        slots_kernel, shape((4, 128), jnp.int32), (), [S, V, V], flops=20_000_000_000, nbytes=70_000, name="slots"
    )(meta, owner.reshape(1, 128), owner)
    answered = call(
        attend_kernel,
        shape((16, 160, LANES)),
        [pltpu.VMEM((256, 4096), F32)],
        [S, S, V, V, V],
        flops=1_000_000_000,
        nbytes=3_000_000,
        name="attend",
    )(meta, slots, mine, twin, mark)
    came = lax.all_to_all(answered, ("x", "y"), 0, 0, tiled=True)
    attention_out, decode_cache = call(
        unpack_kernel,
        [shape((rows, 1024)), shape((128, 2, 1024))],
        (),
        [V],
        nbytes=1_300_000,
        name="unpack",
    )(came)

    reversed_taps = jnp.pad(mr_taps[:, ::-1].astype(F32), ((0, 0), (1, 127)))
    hyena_stream, filter_state = call(
        conv_kernel,
        [shape((rows, channels)), shape((128, channels))],
        [pltpu.VMEM((2, 160, channels), BF16)],
        [S] + [V] * 9,
        flops=100_000_000,
        nbytes=3_000_000,
        name="conv",
    )(meta, reversed_taps, mixed, mr_post, keep, give, got, one, two, rest)
    return hyena_stream, attention_out, decode_cache, filter_state


def solution(mesh):
    fine = Mesh(mesh.devices.reshape(4, 4, 2, 2, 4), (*CTX, "tp"))
    block = P(CTX, "tp")
    in_specs = (block, block, block, P("tp", None), block, block, P("tp", None), block, block, block, P())
    out_specs = (block, block, P(CTX, None, "tp"), block)
    return jax.shard_map(body, mesh=fine, in_specs=in_specs, out_specs=out_specs, check_vma=False)
```

```python
import functools
import math

import jax
import jax.numpy as jnp
from jax import lax
from jax.experimental import pallas as pl
from jax.experimental.pallas import tpu as pltpu
from jax.sharding import Mesh, PartitionSpec as P

HEAD_DIM = 128
CAP = 4
EPS_NORM = 1e-06
MASKED = -1e30
CTX = ("x", "y", "zh", "c")
F32 = jnp.float32
BF16 = jnp.bfloat16
LANES = 128
TILE = 32
TAPS = 7
HALO = 40
PAIRS = tuple((a, b) for a in range(TAPS + 1) for b in range(a, TAPS + 1))


def ctx_route(array, target):
    pairs = [(i, target(i)) for i in range(64) if 0 <= target(i) < 64]
    return lax.ppermute(array, CTX, pairs)


def next_chip(i):
    return 63 if i == 63 else (i + 1 if i % 2 else i - 1)


def across(i):
    return (i + 1 if i % 2 else i - 1) % 64


def second_chip(i):
    return {63: 61, 61: 63}.get(i, i + 3 if i % 2 else i - 3)


SWAP = [(0, 1), (1, 0)]


def call(kernel, out_shape, scratch=(), in_spaces=None, flops=0, nbytes=0, name=None, out_space=pltpu.VMEM, vmem=24):
    specs = [pl.BlockSpec(memory_space=space) for space in in_spaces]
    if isinstance(out_shape, (list, tuple)):
        outs = [pl.BlockSpec(memory_space=pltpu.VMEM) for _ in out_shape]
    else:
        outs = pl.BlockSpec(memory_space=out_space)
    return pl.pallas_call(
        kernel,
        out_shape=out_shape,
        in_specs=specs,
        out_specs=outs,
        scratch_shapes=list(scratch),
        compiler_params=pltpu.CompilerParams(vmem_limit_bytes=vmem * 1024 * 1024),
        cost_estimate=pl.CostEstimate(flops=flops, bytes_accessed=nbytes, transcendentals=0),
        name=name,
    )


V, S = pltpu.VMEM, pltpu.SMEM


def lanes_at(index, width):
    return pl.ds(pl.multiple_of(index * width, width), width)


def halo_rows(meta, far, near, early, step):
    odd = meta[5] == 1
    rows = pl.ds(pl.multiple_of(64 + step // 8 * 16, 16), 16)
    other = far[rows, lanes_at(step % 8, LANES)].astype(F32)
    other = jnp.where(meta[0] == 0, jnp.zeros_like(other), other)
    twin = near[:, lanes_at(step, LANES)].astype(F32)
    before = jnp.where(odd, twin, other)
    after = jnp.where(meta[0] == 63, early, jnp.where(odd, other, twin))
    return before, after


def sum_pairs(out, row, base, tiles, terms_of, packed=None):
    zero = jnp.zeros((8, LANES), F32)
    lane = lax.broadcasted_iota(jnp.int32, (8, LANES), 1)
    packed = zero if packed is None else packed
    for tile in range(tiles):

        def collect(step, sums, tile=tile):
            terms = terms_of(tile, lanes_at(step, LANES))
            return tuple(t + terms[a] * terms[b] for t, (a, b) in zip(sums, PAIRS))

        sums = lax.fori_loop(0, base, collect, (zero,) * len(PAIRS), unroll=4)
        for q, part in enumerate(sums):
            packed = jnp.where(lane == q + 64 * tile, jnp.sum(part, axis=1, keepdims=True), packed)
    out[row : row + 8, :] = packed


def stats_kernel(stream, pre, post, taps, out, us, sf, pf, tf):
    tf[0:TAPS, :] = taps[...].astype(F32)
    chunks = stream.shape[1] // LANES

    def prepare(step, carry):
        cs = lanes_at(step, LANES)
        s = stream[:, cs].astype(F32)
        sf[:, cs] = s
        pf[:, cs] = post[:, cs].astype(F32)
        us[:, cs] = s * pre[:, cs].astype(F32)
        return carry

    lax.fori_loop(0, chunks, prepare, 0, unroll=2)
    out[0:8, :] = jnp.zeros((8, LANES), F32)
    for group in range(1, TILE // 8):

        def terms_of(tile, cs, group=group):
            row = tile * TILE + group * 8
            gate = pf[row : row + 8, cs]
            behind = [us[pl.ds(row - j, 8), cs] for j in range(TAPS)]
            return [sf[row : row + 8, cs]] + [tf[j : j + 1, cs] * gate * behind[j] for j in range(TAPS)]

        sum_pairs(out, group * 8, chunks, 2, terms_of)


def head_kernel(meta, stream, pre, post, taps, far, near, partial, out, us, sf, pf, tf):
    tf[0:TAPS, :] = taps[...].astype(F32)
    chunks = stream.shape[1] // LANES

    def prepare(step, carry):
        cs = lanes_at(step, LANES)
        own = [ref[16:TILE, cs].astype(F32)[8:16] for ref in (stream, pre)]
        halos = halo_rows(meta, far, near, jnp.concatenate(own, axis=0), step)
        squares = []
        for tile in range(2):
            halo = halos[tile]
            rows = slice(tile * TILE, tile * TILE + 16)
            s = stream[rows, cs].astype(F32)[0:8]
            sf[tile, :, cs] = s
            pf[tile, :, cs] = post[rows, cs].astype(F32)[0:8]
            us[tile, 0:8, cs] = halo[0:8] * halo[8:16]
            us[tile, 8:16, cs] = s * pre[rows, cs].astype(F32)[0:8]
            squares.append(carry[tile] + halo[0:8] * halo[0:8])
        return tuple(squares)

    zero = jnp.zeros((8, LANES), F32)
    squares = lax.fori_loop(0, chunks, prepare, (zero, zero), unroll=4)
    lane = lax.broadcasted_iota(jnp.int32, (8, LANES), 1)
    packed = zero
    for tile in range(2):
        packed = jnp.where(lane == HALO + 64 * tile, jnp.sum(squares[tile], axis=1, keepdims=True), packed)

    def terms_of(tile, cs):
        gate = pf[tile, :, cs]
        behind = [us[tile, pl.ds(8 - j, 8), cs] for j in range(TAPS)]
        return [sf[tile, :, cs]] + [tf[j : j + 1, cs] * gate * behind[j] for j in range(TAPS)]

    sum_pairs(out, 0, chunks, 2, terms_of, packed)
    out[8:TILE, :] = partial[8:TILE, :]


def pack_kernel(k, v, far, far_values, q, out):
    for a in range(8):
        cols = slice(a * LANES, (a + 1) * LANES)
        for xb in range(2):
            n = ((a // 4) * 2 + xb) * 4 + a % 4
            out[n, 0:64, :] = k[:, cols]
            out[n, 64:128, :] = v[:, cols]
            out[n, 128:192, :] = far[0:64, cols]
            out[n, 192:256, :] = far_values[:, cols]
            for t in range(2):
                low = TILE * t + 16 * xb
                out[n, 256 + 16 * t : 272 + 16 * t, :] = q[low : low + 16, cols]


def mix_kernel(
    meta, stream, pre, post, mrpre, taps, he, hl, half, other, mixed, keep, give,
    sc, s2, xs, tf,
):
    odd = meta[5] == 1
    tf[0:TAPS, :] = taps[...].astype(F32)
    width = 1.0 / 8192.0
    total = half[...] + other[...]
    scale = lax.rsqrt(total * width + EPS_NORM)
    for tile in range(2):
        near = 64 * tile
        far = near + HALO
        sc[tile, 0:8, :] = jnp.broadcast_to(scale[0:8, far : far + 1], (8, LANES))
        sc[tile, 8:40, :] = jnp.broadcast_to(scale[:, near : near + 1], (TILE, LANES))
    lane = lax.broadcasted_iota(jnp.int32, (TILE, LANES), 1)
    for tile in range(2):
        factor = [jnp.ones((TILE, LANES), F32)]
        for j in range(TAPS):
            factor.append(sc[tile, pl.ds(8 - j, TILE), :])
        weight = jnp.zeros((TILE, LANES), F32)
        for q, (a, b) in enumerate(PAIRS):
            term = factor[a] * factor[b]
            weight = jnp.where(lane == q + 64 * tile, term if a == b else term * 2.0, weight)
        rows = slice(tile * TILE, (tile + 1) * TILE)
        squares = jnp.sum(weight * total, axis=1, keepdims=True)
        second = lax.rsqrt(jnp.maximum(squares, 0.0) * width + EPS_NORM)
        s2[rows, :] = jnp.broadcast_to(second, (TILE, LANES))

    def one(step, carry):
        cs = lanes_at(step, LANES)
        s = stream[:, cs].astype(F32)
        p = pre[:, cs].astype(F32)
        u = s * p
        own = jnp.concatenate([s[TILE - 8 : TILE], p[TILE - 8 : TILE]], axis=0)
        before, after = halo_rows(meta, he, hl, own, step)
        eu, lu = before[0:8] * before[8:16], after[0:8] * after[8:16]
        gate = post[:, cs].astype(F32)
        front = mrpre[:, cs].astype(F32)
        for tile, halo in enumerate((eu, lu)):
            rows = slice(tile * TILE, (tile + 1) * TILE)
            xs[tile, 0:8, :] = (halo * sc[tile, 0:8, :]).astype(BF16).astype(F32)
            xs[tile, 8:40, :] = (u[rows] * sc[tile, 8:40, :]).astype(BF16).astype(F32)
        values = []
        for tile in range(2):
            rows = slice(tile * TILE, (tile + 1) * TILE)
            acc = jnp.zeros((TILE, LANES), F32)
            for j in range(TAPS):
                acc = acc + tf[j : j + 1, cs] * xs[tile, pl.ds(8 - j, TILE), :]
            value = (s[rows] + gate[rows] * acc).astype(BF16)
            mixed[rows, cs] = value
            values.append((front[rows] * value.astype(F32) * s2[rows, :]).astype(BF16))
        keep[:, cs] = jnp.where(odd, values[0], values[1])
        give[:, cs] = jnp.where(odd, values[1], values[0])
        return carry

    lax.fori_loop(0, stream.shape[1] // LANES, one, 0, unroll=2)


def conv_kernel(meta, taps, mixed, post, keep, give, got, one, two, rest, out, state, ext):
    ext[0, 0:32, :] = two[32:64, :]
    ext[0, 32:64, :] = two[0:32, :]
    ext[0, 64:96, :] = one[32:64, :]
    ext[0, 96:128, :] = one[0:32, :]
    ext[0, 128:160, :] = give[...]
    ext[1, 0:32, :] = rest[64:96, :]
    ext[1, 32:64, :] = rest[32:64, :]
    ext[1, 64:96, :] = rest[0:32, :]
    ext[1, 96:128, :] = got[...]
    ext[1, 128:160, :] = keep[...]
    group_width = out.shape[1] // taps.shape[0]
    for g in range(taps.shape[0]):
        row = jnp.broadcast_to(taps[g : g + 1, :], (TILE, 256))
        toeplitz = pltpu.roll(row, 0, 1, stride=1, stride_axis=0)[:, 0:160].astype(BF16)
        cols = slice(g * group_width, (g + 1) * group_width)
        for part in range(2):
            place = meta[5] if part == 0 else 1 - meta[5]
            rows = pl.ds(pl.multiple_of(place * TILE, TILE), TILE)
            acc = jnp.dot(toeplitz, ext[part, :, cols], preferred_element_type=F32)
            value = mixed[rows, cols].astype(F32) + post[rows, cols].astype(F32) * acc
            out[rows, cols] = value.astype(BF16)

    @pl.when(meta[0] == 0)
    def _():
        state[...] = ext[1, 32:160, :]

    @pl.when(meta[0] != 0)
    def _():
        state[...] = jnp.zeros_like(state)


def slots_kernel(meta, owner_row, owner_col, out):
    xb, zh, c = meta[2], meta[4], meta[5]
    row = lax.broadcasted_iota(jnp.int32, (128, 128), 0)
    col = lax.broadcasted_iota(jnp.int32, (128, 128), 1)
    mine = owner_col[...]
    before = (owner_row[...] == mine) & (col < row)
    rank = jnp.sum(jnp.where(before, 1, 0), axis=1, keepdims=True)
    want = (col // 2 * 4 + zh * 2 + c) * CAP + xb * 2 + col % 2
    found = (mine * CAP + rank == want) & (col < 32)
    tile = jnp.sum(jnp.where(found, row + 1, 0), axis=0, keepdims=True) - 1
    held = jnp.maximum(tile, 0)
    late = held >= 64
    device = jnp.where(late, 127 - held, held)
    across_z = (device >> 1 & 1) != zh
    holder = jnp.where(across_z, (device + jnp.where(device & 1 == 1, 1, 63)) & 63, device)
    out[0:1, :] = holder >> 2
    out[1:2, :] = jnp.where(across_z, 128, 0) + jnp.where(late, TILE, 0)
    out[2:3, :] = jnp.where((holder & 1) == c, 1, 0)
    out[3:4, :] = jnp.where(tile >= 0, 1, 0)


def attend_kernel(meta, slots, mine, twin, after, out, scores):
    xb, zh, c = meta[2], meta[4], meta[5]

    def pieces(n, carry):
        for slot in range(2):
            at = n * 2 + slot
            src, low = slots[0, at], slots[1, at]
            near, there = slots[2, at] == 1, slots[3, at] == 1
            for kv in range(2):
                rows = pl.ds(pl.multiple_of(low + 64 * kv, TILE), TILE)
                value = jnp.where(near, mine[src, rows, :], twin[src, rows, :])
                value = jnp.where(there, value, jnp.zeros_like(value))
                first = 32 + (slot * 2 + kv) * TILE
                out[n, first : first + TILE, :] = value
        return carry

    lax.fori_loop(0, 16, pieces, 0, unroll=16)
    log_scale = math.log2(math.e) / math.sqrt(HEAD_DIM)
    def owner(core, far):
        def of(src):
            device = src * 4 + zh * 2 + core
            return (jnp.where(core == 1, device + 1, device + 63) % 64) if far else device

        return of

    groups = [(ref, 128 * far, owner(core, far)) for ref, core in ((mine, c), (twin, 1 - c)) for far in range(2)]

    def place(device, late, u):
        return (127 - device if late else device) * TILE + u

    def columns(late):
        col = lax.broadcasted_iota(jnp.int32, (1, 512), 1)
        return [place(of(col // TILE), late, col % TILE) for _, _, of in groups]

    def tiles(ref, low, count):
        return ref[:, low : low + count, :].reshape(16 * count, LANES)

    block = 256
    places = (columns(False), columns(True))
    for late in range(2):
        for part in range(256 // block):
            src0 = part * (block // 16)
            query = mine[src0 : src0 + block // 16, 256 + 16 * late : 272 + 16 * late, :]
            query = query.reshape(block, LANES)
            row = lax.broadcasted_iota(jnp.int32, (block, 1), 0)
            spot = place((src0 + row // 16) * 4 + zh * 2 + c, bool(late), xb * 16 + row % 16)
            top = jnp.full((block, LANES), MASKED, F32)
            jobs = []
            for key_late in range(late + 1):
                for g, (ref, low, _) in enumerate(groups):
                    jobs.append((len(jobs), key_late, g, ref, low + TILE * key_late))
            for n, key_late, g, ref, low in jobs:
                keys = tiles(ref, low, TILE)
                found = lax.dot_general(
                    query, keys, (((1,), (1,)), ((), ())), preferred_element_type=F32
                )
                if key_late == late:
                    found = jnp.where(places[key_late][g] <= spot, found, MASKED)
                scores[:, n * 512 : (n + 1) * 512] = found
                for k in range(4):
                    top = jnp.maximum(top, found[:, k * LANES : (k + 1) * LANES])
            top = jnp.max(top, axis=1, keepdims=True)
            total = jnp.zeros((block, LANES), F32)
            summed = jnp.zeros((block, LANES), F32)
            for n, key_late, g, ref, low in jobs:
                weights = jnp.exp2((scores[:, n * 512 : (n + 1) * 512] - top) * log_scale)
                for k in range(4):
                    total = total + weights[:, k * LANES : (k + 1) * LANES]
                values = tiles(ref, low + 64, TILE)
                summed = summed + jnp.dot(
                    weights.astype(BF16), values, preferred_element_type=F32
                )
            result = (summed / jnp.sum(total, axis=1, keepdims=True)).astype(BF16)
            out[src0 : src0 + block // 16, 16 * late : 16 * late + 16, :] = result.reshape(
                block // 16, 16, LANES
            )


def unpack_kernel(came, att, cache):
    for n in range(16):
        xa, xb, y = n // 8, (n // 4) % 2, n % 4
        a = xa * 4 + y
        cols = slice(a * LANES, (a + 1) * LANES)
        att[16 * xb : 16 * xb + 16, cols] = came[n, 0:16, :]
        att[TILE + 16 * xb : TILE + 16 * xb + 16, cols] = came[n, 16:32, :]
        for slot in range(2):
            rows = slice((xb * 2 + slot) * TILE, (xb * 2 + slot + 1) * TILE)
            low = 32 + slot * 2 * TILE
            cache[rows, 0, cols] = came[n, low : low + TILE, :]
            cache[rows, 1, cols] = came[n, low + TILE : low + 2 * TILE, :]


def shape(dims, dtype=BF16):
    return jax.ShapeDtypeStruct(dims, dtype)


def body(stream, se_pre, se_post, se_taps, mr_pre, mr_post, mr_taps, query, key, value, owner):
    x, y, zh, c = (lax.axis_index(name) for name in CTX)
    me = ((x * 4 + y) * 2 + zh) * 2 + c
    meta = jnp.stack([me, x // 2, x % 2, y, zh, c, c, c]).astype(jnp.int32)
    rows, channels = stream.shape

    odd = c == 1
    early_raw = jnp.concatenate([stream[24:32], se_pre[24:32]], axis=0)
    late_raw = jnp.concatenate([stream[56:64], se_pre[56:64]], axis=0)
    outer = jnp.where(odd, early_raw, late_raw)
    halo_near = lax.ppermute(jnp.where(odd, late_raw, early_raw), "c", SWAP)
    far = ctx_route(jnp.concatenate([key, outer[:, :1024], outer[:, 1024:]], axis=0), across)
    held, halo_near = lax.optimization_barrier((value, halo_near))
    far_values = ctx_route(held, across)
    taps = se_taps.T
    partial = call(
        stats_kernel,
        shape((TILE, LANES), F32),
        [pltpu.VMEM((rows, channels), F32)] * 3 + [pltpu.VMEM((8, channels), F32)],
        [V] * 4,
        flops=15_000_000,
        nbytes=800_000,
        name="stats",
    )(stream, se_pre, se_post, taps)
    sums = call(
        head_kernel,
        shape((TILE, LANES), F32),
        [pltpu.VMEM((2, 16, channels), F32)] + [pltpu.VMEM((2, 8, channels), F32)] * 2 + [pltpu.VMEM((8, channels), F32)],
        [S] + [V] * 7,
        flops=5_000_000,
        nbytes=300_000,
        name="head",
    )(meta, stream, se_pre, se_post, taps, far, halo_near, partial)
    half = sums + lax.ppermute(sums, "tp", [(i, i ^ 1) for i in range(4)])
    packed, half = lax.optimization_barrier((far_values, half))
    other = lax.ppermute(half, "tp", [(i, i ^ 2) for i in range(4)])
    mixed, keep, give = call(
        mix_kernel,
        [shape((rows, channels)), shape((TILE, channels)), shape((TILE, channels))],
        [pltpu.VMEM((2, 40, LANES), F32), pltpu.VMEM((64, LANES), F32), pltpu.VMEM((2, 40, LANES), F32)]
        + [pltpu.VMEM((8, channels), F32)],
        [S] + [V] * 9,
        flops=20_000_000_000,
        nbytes=3_500_000,
        name="mix",
    )(meta, stream, se_pre, se_post, mr_pre, taps, far, halo_near, half, other)

    got = lax.ppermute(give, "c", SWAP)
    pair = jnp.concatenate([keep, got], axis=0)
    heads = call(
        pack_kernel, shape((16, 288, LANES)), (), [V] * 5, nbytes=2_000_000, name="pack"
    )(key, value, far, packed, query)
    mine = lax.all_to_all(heads, ("x", "y"), 0, 0, tiled=True)
    two = ctx_route(pair, second_chip)
    one = ctx_route(pair, next_chip)
    mark = pair[:16, :128]
    mine, pair = lax.optimization_barrier((mine, pair))
    share = jnp.concatenate([one, two[:TILE]], axis=0)

    rest = lax.ppermute(share, "c", SWAP)
    twin = lax.ppermute(mine, "c", [(0, 1), (1, 0)])

    slots = call(
        slots_kernel, shape((4, 128), jnp.int32), (), [S, V, V], flops=20_000_000_000, nbytes=70_000, name="slots"
    )(meta, owner.reshape(1, 128), owner)
    answered = call(
        attend_kernel,
        shape((16, 160, LANES)),
        [pltpu.VMEM((256, 4096), F32)],
        [S, S, V, V, V],
        flops=1_000_000_000,
        nbytes=3_000_000,
        name="attend",
    )(meta, slots, mine, twin, mark)
    came = lax.all_to_all(answered, ("x", "y"), 0, 0, tiled=True)
    attention_out, decode_cache = call(
        unpack_kernel,
        [shape((rows, 1024)), shape((128, 2, 1024))],
        (),
        [V],
        nbytes=1_300_000,
        name="unpack",
    )(came)

    reversed_taps = jnp.pad(mr_taps[:, ::-1].astype(F32), ((0, 0), (1, 127)))
    hyena_stream, filter_state = call(
        conv_kernel,
        [shape((rows, channels)), shape((128, channels))],
        [pltpu.VMEM((2, 160, channels), BF16)],
        [S] + [V] * 9,
        flops=100_000_000,
        nbytes=3_000_000,
        name="conv",
    )(meta, reversed_taps, mixed, mr_post, keep, give, got, one, two, rest)
    return hyena_stream, attention_out, decode_cache, filter_state


def solution(mesh):
    fine = Mesh(mesh.devices.reshape(4, 4, 2, 2, 4), (*CTX, "tp"))
    block = P(CTX, "tp")
    in_specs = (block, block, block, P("tp", None), block, block, P("tp", None), block, block, block, P())
    out_specs = (block, block, P(CTX, None, "tp"), block)
    return jax.shard_map(body, mesh=fine, in_specs=in_specs, out_specs=out_specs, check_vma=False)
```
